32 devices in a mesh: groups: 2 (over x), dev: 16 (over z, y, core).
Axes of the slice: x: 2, y: 2, z: 4, core: 2. Of those that a mesh axis runs over, the one named last changes fastest.
Arguments:
- hidden_in: bfloat16 [512, 4096], P(('groups', 'dev')), parts along dimension 0, may hold values from -2 to 2
- queries: bfloat16 [512, 4096], P(('groups', 'dev')), parts along dimension 0, may hold values from -80 to 80
- fresh_key_value: bfloat16 [512, 2, 256], P(('groups', 'dev')), parts along dimension 0, may hold values from -6 to 6
- segment_key_cache: bfloat16 [4096, 16, 256], P(('groups', 'dev')), parts along dimension 0, may hold values from -6 to 6
- segment_value_cache: bfloat16 [4096, 16, 256], P(('groups', 'dev')), parts along dimension 0, may hold values from -6 to 6
- segment_owner_row: int32 [4096], P(('groups', 'dev')), parts along dimension 0, may hold values from 0 to 255, as said below
- segment_length: int32 [4096], P(('groups', 'dev')), parts along dimension 0, may hold values from 1 to 16
- expert_ids: int32 [512, 8], P(('groups', 'dev')), parts along dimension 0, may hold values from 0 to 15, all different within a row; in each aligned block of 16 rows (0 to 15, 16 to 31, ...) at most 8 rows name the same one
- gate_score: int32 [512, 8], P(('groups', 'dev')), parts along dimension 0, may hold values from 0 to 11
- out_proj: bfloat16 [4096, 4096], P('dev'), may hold values from -0.09375 to 0.09375
- norm_gain: bfloat16 [4096], replicated, may hold values from 0.099609375 to 1.8984375
- w_gate: bfloat16 [16, 4096, 768], P('dev'), may hold values from -0.09375 to 0.09375
- w_up: bfloat16 [16, 4096, 768], P('dev'), may hold values from -0.09375 to 0.09375
- w_down: bfloat16 [16, 768, 4096], P('dev'), may hold values from -0.21875 to 0.21875
Outputs:
- layer_out: bfloat16 [512, 4096], P(('groups', 'dev')), parts along dimension 0
The draws below stay inside these ranges and needn't reach their ends.
There are 2 independent parts, one for each index of `groups`. The reference program is written for one: setup_inputs(seed, part) draws one part's arguments, and reference() takes and returns one part's arrays. A program takes and returns all parts, laid end to end along the dimension named above; an argument that names none is the same for every part. Nothing has to cross between parts.
Inputs may be any that keep to these rules, and one draw needn't show every extreme that they name: `segment_owner_row`: segment rows never fall along the segments, and every row owns at least one segment. `expert_ids`: each row names 8 different experts; among the rows of one device no expert is named by more than 8 rows.
All inputs are finite; a program needn't handle non-finite values.
Results may differ from the reference program's by a relative error of at most 0.024.
Values may be sent and summed in bfloat16 or wider, within the bound.
A program may use at most 128 MiB of HBM per device.

```python
import math
import jax
import jax.numpy as jnp
import numpy as np
from jax import lax

D = 4096
HEAD_SIZE = 128
TOP = 8
HQ = 32
KEY_VALUE_HEADS = 2
FF = 768
SEGMENT_SLOTS = 16
ROW_DEV = 16
DEVICE_SEGMENTS = 128
DECODE_ROWS = 256
CACHE_SEGMENTS = 2048
EXPERTS = 16
CAP = 8
HPD = 2
N_DEV = 16


def draw_queries(key, part):
    base_values = jnp.clip(jax.random.normal(key, (DECODE_ROWS, HQ * HEAD_SIZE), jnp.float32), -5.0, 5.0)
    return base_values.astype(jnp.bfloat16)


def split_runs(key, length, count):
    cut_points = jnp.sort(jax.random.permutation(key, length - 1)[:count - 1].astype(jnp.int32) + 1)
    positions = jnp.arange(length, dtype=jnp.int32)
    return jnp.sum((positions[:, None] >= cut_points[None, :]).astype(jnp.int32), axis=1).astype(jnp.int32)


def draw_segment_owner_row(key, part):
    half_devices = N_DEV // 2
    head_length = half_devices * DEVICE_SEGMENTS + 1
    middle_length = DEVICE_SEGMENTS - 1
    tail_length = CACHE_SEGMENTS - (half_devices + 1) * DEVICE_SEGMENTS
    head_rows = jnp.zeros((head_length,), jnp.int32)
    middle_rows = 1 + split_runs(jax.random.fold_in(key, 11), middle_length, ROW_DEV - 1)
    tail_rows = ROW_DEV + split_runs(jax.random.fold_in(key, 13), tail_length, DECODE_ROWS - ROW_DEV)
    return jnp.concatenate([head_rows, middle_rows.astype(jnp.int32), tail_rows.astype(jnp.int32)]).astype(jnp.int32)


def set_ends(entries, rng, low, top_value):
    extent = entries.shape
    spot = [jax.random.randint(jax.random.fold_in(rng, axis), (), 0, extent[axis]) for axis in range(len(extent))]
    entries = entries.at[tuple(spot)].set(low)
    longest = extent.index(max(extent))
    spot[longest] = (spot[longest] + 1) % extent[longest]
    return entries.at[tuple(spot)].set(top_value)


def level_of(key, dims, cuts, least, largest):
    def one(dim, shards_of):
        draws = jax.random.uniform(jax.random.fold_in(jax.random.fold_in(key, 6), dim), (shards_of,), jnp.float32, least / len(cuts), largest / len(cuts))
        return jnp.repeat(jnp.exp(draws), dims[dim] // shards_of).reshape((-1,) + (1,) * (len(dims) - dim - 1))

    gain = one(*cuts[0])
    for cut in cuts[1:]:
        gain = gain * one(*cut)
    return gain


def assign_block(stream_key, own, number, rows, amount, top, reach, lean):
    order = jax.random.permutation(stream_key, amount)
    heavy_load, usual = portions_of(amount, rows * top, reach, lean, True), portions_of(amount, rows * top, reach, lean, False)
    places = jnp.arange(amount)

    def named(tallies, turn):
        used = int((tallies > 0).sum())
        fixed = max(1, used // 4)
        shifted = fixed + (places - fixed + turn * (used - fixed)) % max(1, amount - fixed)
        return jnp.zeros((amount,), jnp.int32).at[order[jnp.where(places < fixed, places, shifted)]].set(jnp.asarray(tallies, jnp.int32))

    tallies = jnp.where(number % 4 == 0, named(heavy_load, number // 4), named(usual, number - number // 4 - 1))
    mixed = jax.random.permutation(jax.random.fold_in(own, 3), amount)
    donor, sink = mixed[0:amount // 2 * 2:2], mixed[1:amount // 2 * 2:2]
    room = jnp.minimum(tallies[donor] - 1, reach - tallies[sink]) // 2
    room = jnp.where((donor == order[0]) | (sink == order[0]) | (tallies[sink] == 0), 0, jnp.maximum(room, 0))
    shifted = jax.random.randint(jax.random.fold_in(own, 4), (amount // 2,), 0, 1 << 20) % (room + 1)
    tallies = tallies.at[donor].add(-shifted).at[sink].add(shifted)
    items = jnp.searchsorted(jnp.cumsum(tallies), jnp.arange(rows * top), side="right").astype(jnp.int32)
    listing = items.reshape(top, rows).T
    listing = listing[jax.random.permutation(jax.random.fold_in(own, 1), rows)]
    turn = jax.random.randint(jax.random.fold_in(own, 2), (rows, 1), 0, top)
    return jnp.take_along_axis(listing, (jnp.arange(top)[None, :] + turn) % top, axis=1)


def portions_of(count, total, most, skew, full):
    weights = [(1 << 20) // math.isqrt(grade ** skew) + 1 for grade in range(1, count + 1)]
    largest = most if full else min(most, max(-(-total // count), total * weights[0] // sum(weights)))
    least = 1 if total - largest >= count - 1 else 0
    given, surplus = [largest] + [least] * (count - 1), total - largest - least * (count - 1)
    while surplus > 0:
        movable = [i for i in range(1, count) if given[i] < largest] or [i for i in range(1, count) if given[i] < most]
        mass, left = sum([weights[i] for i in movable]), surplus
        for i in movable:
            extra = min(most - given[i], max(1, left * weights[i] // mass), surplus)
            given[i] = given[i] + extra
            surplus = surplus - extra
    return np.array(given)


def noise(key, shape, spread, reach, shards=(), kind=jnp.bfloat16):
    values = jax.random.normal(key, shape, jnp.float32) * spread
    if len(shards) > 0:
        values = level_of(key, shape, shards, -0.22, 0.18) * values
    return jnp.clip(values, min=-reach, max=reach).astype(kind)


def setup_inputs(seed: int = 0, part: int = 0) -> dict:
    key_list = jax.random.split(jax.random.key(seed), 15)
    part_splits = jax.random.split(jax.random.fold_in(key_list[14], part), 15)
    hidden_in = noise(part_splits[0], (DECODE_ROWS, D), 0.3, 2.0, ((0, 16),))
    queries = draw_queries(jax.random.fold_in(jax.random.fold_in(key_list[14], part), 71), part)
    fresh_key_value = noise(part_splits[2], (DECODE_ROWS, 2, KEY_VALUE_HEADS * HEAD_SIZE), 1.0, 6.0, ((0, 16),))
    segment_key_cache = noise(part_splits[3], (CACHE_SEGMENTS, SEGMENT_SLOTS, KEY_VALUE_HEADS * HEAD_SIZE), 1.0, 6.0, ((0, 16),))
    segment_value_cache = noise(part_splits[4], (CACHE_SEGMENTS, SEGMENT_SLOTS, KEY_VALUE_HEADS * HEAD_SIZE), 1.0, 6.0, ((0, 16),))
    segment_owner_row = draw_segment_owner_row(jax.random.fold_in(jax.random.fold_in(key_list[14], part), 71), part)
    segment_length = set_ends(jax.random.randint(part_splits[6], (CACHE_SEGMENTS,), 1, SEGMENT_SLOTS + 1), jax.random.fold_in(part_splits[6], 1), 1, SEGMENT_SLOTS).astype(jnp.int32)
    expert_ids_keys = jax.random.split(jax.random.fold_in(part_splits[7], 1), DECODE_ROWS // ROW_DEV)
    expert_ids_turns = jax.random.permutation(jax.random.fold_in(part_splits[7], 3), DECODE_ROWS // ROW_DEV)
    expert_ids = jax.vmap(lambda own, number: assign_block(jax.random.fold_in(part_splits[7], 2), own, number, ROW_DEV, EXPERTS, TOP, CAP, 2))(expert_ids_keys, expert_ids_turns).reshape((DECODE_ROWS, TOP))
    gate_score = set_ends(jax.random.randint(part_splits[8], (DECODE_ROWS, TOP), 0, 12), jax.random.fold_in(part_splits[8], 1), 0, 11).astype(jnp.int32)
    out_proj = noise(key_list[9], (HQ * HEAD_SIZE, D), (HQ * HEAD_SIZE) ** -0.5, 0.09375, ((0, 16),))
    norm_gain = jnp.clip(1.0 + 0.18 * jax.random.normal(key_list[10], (D,), jnp.float32), 0.099609375, 1.8984375).astype(jnp.bfloat16)
    w_gate = noise(key_list[11], (EXPERTS, D, FF), D ** -0.5, 0.09375, ((0, 16),))
    w_up = noise(key_list[12], (EXPERTS, D, FF), D ** -0.5, 0.09375, ((0, 16),))
    w_down = noise(key_list[13], (EXPERTS, FF, D), FF ** -0.5, 0.21875, ((0, 16),))
    return dict(hidden_in=hidden_in, queries=queries, fresh_key_value=fresh_key_value, segment_key_cache=segment_key_cache, segment_value_cache=segment_value_cache, segment_owner_row=segment_owner_row, segment_length=segment_length, expert_ids=expert_ids, gate_score=gate_score, out_proj=out_proj, norm_gain=norm_gain, w_gate=w_gate, w_up=w_up, w_down=w_down)


FLOOR_MAX = -1e+30

def segment_terms(query_rows, key_cache, value_cache, seg_lengths):
    seg_count = key_cache.shape[0]
    seg_width = key_cache.shape[1]
    kv_heads = key_cache.shape[2] // HEAD_SIZE
    group_size = HQ // kv_heads
    query_blocks = query_rows.reshape(seg_count, kv_heads, group_size, HEAD_SIZE).astype(jnp.float32)
    key_blocks = key_cache.reshape(seg_count, seg_width, kv_heads, HEAD_SIZE).astype(jnp.float32)
    value_blocks = value_cache.reshape(seg_count, seg_width, kv_heads, HEAD_SIZE).astype(jnp.float32)
    scores = jnp.einsum('skgd,stkd->skgt', query_blocks, key_blocks) * HEAD_SIZE ** (-0.5)
    live_slots = jnp.arange(seg_width, dtype=jnp.int32)[None, None, None, :] < seg_lengths[:, None, None, None]
    scores = jnp.where(live_slots, scores, -jnp.inf)
    seg_max = lax.optimization_barrier(jnp.max(scores, axis=3))
    prob_rows = jnp.exp(scores - seg_max[..., None])
    seg_sum = lax.optimization_barrier(jnp.sum(prob_rows, axis=3))
    rounded = lax.optimization_barrier(prob_rows.astype(jnp.bfloat16)).astype(jnp.float32)
    seg_out = jnp.einsum('skgt,stkd->skgd', rounded, value_blocks)
    return (seg_max.reshape(seg_count, HQ), seg_sum.reshape(seg_count, HQ), seg_out.reshape(seg_count, HQ, HEAD_SIZE))

def reduce_rows(seg_max, seg_sum, seg_out, row_ids, row_count):
    row_max = jax.ops.segment_max(seg_max, row_ids, num_segments=row_count)
    weight = jnp.exp(seg_max - jnp.take(row_max, row_ids, axis=0))
    row_sum = jax.ops.segment_sum(seg_sum * weight, row_ids, num_segments=row_count)
    row_out = jax.ops.segment_sum(seg_out * weight[..., None], row_ids, num_segments=row_count)
    return (row_max, row_sum, row_out)

def fold_own(row_max, row_sum, row_out, query_own, kv_own):
    row_count = query_own.shape[0]
    kv_heads = kv_own.shape[2] // HEAD_SIZE
    group_size = HQ // kv_heads
    query_blocks = query_own.reshape(row_count, kv_heads, group_size, HEAD_SIZE).astype(jnp.float32)
    new_key = kv_own[:, 0].reshape(row_count, kv_heads, 1, HEAD_SIZE).astype(jnp.float32)
    new_value = kv_own[:, 1].reshape(row_count, kv_heads, 1, HEAD_SIZE).astype(jnp.float32)
    own_score = lax.optimization_barrier(jnp.sum(query_blocks * new_key, axis=3)).reshape(row_count, HQ) * HEAD_SIZE ** (-0.5)
    merged = jnp.maximum(row_max, own_score)
    old_weight = jnp.exp(row_max - merged)
    new_weight = jnp.exp(own_score - merged)
    total_sum = row_sum * old_weight + new_weight
    value_term = jnp.broadcast_to(new_value, (row_count, kv_heads, group_size, HEAD_SIZE)).reshape(row_count, HQ, HEAD_SIZE)
    merged_out = row_out * old_weight[..., None] + value_term * new_weight[..., None]
    return (merged, total_sum, merged_out)

def finish(row_max, row_sum, row_out):
    floored = jnp.maximum(row_sum, 1.0)
    block_lse = row_max + jnp.log(floored)
    block_share = (row_out / floored[..., None]).astype(jnp.bfloat16)
    return (block_lse, block_share)

def reference(hidden_in, queries, fresh_key_value, segment_key_cache, segment_value_cache, segment_owner_row, segment_length, expert_ids, gate_score, out_proj, norm_gain, w_gate, w_up, w_down):
    row_total = ROW_DEV * N_DEV

    def block_step(carry_state, block_data):
        best_lse, denominator, numerator = carry_state
        key_block, value_block, row_block, len_block, block_index = block_data
        own_first = (block_index * ROW_DEV).astype(jnp.int32)
        query_rows = jnp.take(queries, row_block, axis=0)
        seg_max, seg_sum, seg_out = segment_terms(query_rows, key_block, value_block, len_block)
        row_max, row_sum, row_out = reduce_rows(seg_max, seg_sum, seg_out, row_block, row_total)
        query_own = lax.dynamic_slice_in_dim(queries, own_first, ROW_DEV, 0)
        kv_own = lax.dynamic_slice_in_dim(fresh_key_value, own_first, ROW_DEV, 0)
        own_max, own_sum, own_out = fold_own(lax.dynamic_slice_in_dim(row_max, own_first, ROW_DEV, 0), lax.dynamic_slice_in_dim(row_sum, own_first, ROW_DEV, 0), lax.dynamic_slice_in_dim(row_out, own_first, ROW_DEV, 0), query_own, kv_own)
        row_max = lax.dynamic_update_slice_in_dim(row_max, own_max, own_first, 0)
        row_sum = lax.dynamic_update_slice_in_dim(row_sum, own_sum, own_first, 0)
        row_out = lax.dynamic_update_slice_in_dim(row_out, own_out, own_first, 0)
        block_lse, block_share = finish(row_max, row_sum, row_out)
        share_f32 = lax.optimization_barrier(block_share).astype(jnp.float32)
        fresh_max = jnp.maximum(best_lse, block_lse)
        old_weight = jnp.exp(best_lse - fresh_max)
        new_weight = jnp.exp(block_lse - fresh_max)
        return ((fresh_max, denominator * old_weight + new_weight, numerator * old_weight[..., None] + share_f32 * new_weight[..., None]), None)
    initial = (jnp.full((row_total, HQ), FLOOR_MAX, jnp.float32), jnp.zeros((row_total, HQ), jnp.float32), jnp.zeros((row_total, HQ, HEAD_SIZE), jnp.float32))
    layer_block_inputs = (segment_key_cache.reshape(N_DEV, DEVICE_SEGMENTS, SEGMENT_SLOTS, KEY_VALUE_HEADS * HEAD_SIZE), segment_value_cache.reshape(N_DEV, DEVICE_SEGMENTS, SEGMENT_SLOTS, KEY_VALUE_HEADS * HEAD_SIZE), segment_owner_row.reshape(N_DEV, DEVICE_SEGMENTS), segment_length.reshape(N_DEV, DEVICE_SEGMENTS), jnp.arange(N_DEV, dtype=jnp.int32))
    final_state, unused = lax.scan(block_step, initial, layer_block_inputs)
    attention = (final_state[2] / final_state[1][..., None]).astype(jnp.bfloat16).reshape(row_total, HQ * HEAD_SIZE)
    per_group = HPD * HEAD_SIZE
    attention_parts = attention.reshape(row_total, N_DEV, per_group).transpose(1, 0, 2)
    weight_parts = out_proj.reshape(N_DEV, per_group, D)

    def project_step(running, pair_items):
        group_part = jnp.dot(pair_items[0], pair_items[1], preferred_element_type=jnp.float32).astype(jnp.bfloat16)
        return (running + lax.optimization_barrier(group_part).astype(jnp.float32), None)
    projected, unused = lax.scan(project_step, jnp.zeros((row_total, D), jnp.float32), (attention_parts, weight_parts))
    mixed = (hidden_in.astype(jnp.float32) + projected).astype(jnp.bfloat16)
    mixed_f32 = mixed.astype(jnp.float32)
    normed = (mixed_f32 * lax.rsqrt(lax.optimization_barrier(jnp.mean(mixed_f32 * mixed_f32, axis=1, keepdims=True)) + 1e-06) * norm_gain.astype(jnp.float32)).astype(jnp.bfloat16)
    gate_probs = jnp.exp(gate_score.astype(jnp.float32) / 4.0)
    gate_probs = gate_probs / lax.optimization_barrier(jnp.sum(gate_probs, axis=1, keepdims=True))
    row_limit = N_DEV * CAP

    def expert_step(running, block_data):
        gate_weight, up_weight, down_weight, expert_index = block_data
        chosen = expert_ids == expert_index
        picked = jnp.any(chosen, axis=1)
        weight = lax.optimization_barrier(jnp.sum(jnp.where(chosen, gate_probs, 0.0), axis=1))
        row_order = jnp.argsort(jnp.where(picked, 0, 1).astype(jnp.int32), stable=True)[:row_limit].astype(jnp.int32)
        tokens = jnp.take(normed, row_order, axis=0)
        gate_proj = jnp.dot(tokens, gate_weight, preferred_element_type=jnp.float32)
        up_proj = jnp.dot(tokens, up_weight, preferred_element_type=jnp.float32)
        activated = (jax.nn.silu(gate_proj) * up_proj).astype(jnp.bfloat16)
        result = jnp.dot(activated, down_weight, preferred_element_type=jnp.float32).astype(jnp.bfloat16)
        result = lax.optimization_barrier(result).astype(jnp.float32)
        return (running.at[row_order].add(result * jnp.take(weight, row_order, axis=0)[:, None]), None)
    moe_sum, unused = lax.scan(expert_step, jnp.zeros((row_total, D), jnp.float32), (w_gate, w_up, w_down, jnp.arange(EXPERTS, dtype=jnp.int32)))
    return (mixed_f32 + moe_sum).astype(jnp.bfloat16)
```

```python
import functools

import jax
import jax.numpy as jnp
from jax import lax
from jax.experimental import pallas as pl
from jax.experimental.pallas import tpu as pltpu
from jax.sharding import PartitionSpec as P

HEAD_SIZE = 128
HQ = 32
LANES = 128
BLOCK_SEGS = 16
LOW = -1e30
F32 = jnp.float32
BF16 = jnp.bfloat16


def halves(width):
    if width % (2 * LANES) == 0:
        return [(0, width // 2), (width // 2, width // 2)]
    return [(0, width)]


def bit_orders(levels):
    first = list(range(levels))
    second = list(first)
    if levels >= 4:
        second[1], second[2] = second[2], second[1]
    return [first, second]


def layer_kernel(
    dims,
    hidden_ref,
    query_ref,
    fresh_ref,
    key_hbm,
    value_hbm,
    owner_ref,
    bias_ref,
    gates_ref,
    proj_hbm,
    gain_ref,
    wg_hbm,
    wu_hbm,
    wd_hbm,
    out_ref,
    key_v,
    value_v,
    proj_v,
    wg_v,
    wu_v,
    wd_v,
    load_sem,
    gathered,
    gate_all,
    seg_query,
    seg_out,
    table,
    table_in,
    lse_tab,
    lse_in,
    part,
    part_in,
    normed_all,
    act_v,
    send_sem,
    recv_sem,
):
    n, levels, row_dev, model, ff, segs, slots, kv_heads, per_dev, pos, pos_lanes = dims
    rows = n * row_dev
    group_size = HQ // kv_heads
    hd = HQ * HEAD_SIZE
    own_cols = per_dev * HEAD_SIZE
    me = lax.axis_index("dev")
    orders = bit_orders(levels)

    def my_bit(k):
        return lax.rem(lax.div(me, 2**k), 2)

    def partner(k):
        return me + (1 - 2 * my_bit(k)) * 2**k

    def axis_of(k):
        return levels - 1 - k

    def static_index(d):
        return tuple((d // 2**k) % 2 for k in reversed(range(levels)))

    mine = tuple(my_bit(k) for k in reversed(range(levels)))

    loads = []
    for i, (src, dst) in enumerate(
        [
            (key_hbm, key_v),
            (value_hbm, value_v),
            (proj_hbm, proj_v),
            (wg_hbm.at[0], wg_v),
            (wu_hbm.at[0], wu_v),
            (wd_hbm.at[0], wd_v),
        ]
    ):
        copy = pltpu.make_async_copy(src, dst, load_sem.at[i])
        copy.start()
        loads.append(copy)

    barrier = pltpu.get_barrier_semaphore()
    for k in range(levels):
        pl.semaphore_signal(
            barrier, inc=1, device_id={"dev": partner(k)}, device_id_type=pl.DeviceIdType.MESH
        )
    pl.semaphore_wait(barrier, levels)

    def remote(src, dst, phase, piece, step, bit):
        copy = pltpu.make_async_remote_copy(
            src_ref=src,
            dst_ref=dst,
            send_sem=send_sem.at[phase, piece, step],
            recv_sem=recv_sem.at[phase, piece, step],
            device_id={"dev": partner(bit)},
            device_id_type=pl.DeviceIdType.MESH,
        )
        copy.start()
        return copy

    def gather(pieces):
        copies = []
        pending = [None] * len(pieces)
        for step in range(levels):
            for i, (buf, c0, width, order, phase, piece) in enumerate(pieces):
                down = order[::-1]
                if pending[i] is not None:
                    pending[i].wait_recv()
                index = [slice(None)] * levels
                for k in down[step:]:
                    index[axis_of(k)] = my_bit(k)
                ref = buf.at[tuple(index) + (slice(None), pl.ds(c0, width))]
                pending[i] = remote(ref, ref, phase, piece, step, down[step])
                copies.append(pending[i])
        for copy in pending:
            copy.wait_recv()
        for copy in copies:
            copy.wait_send()

    def scatter_sum(pieces):
        copies = []
        pending = [None] * len(pieces)

        def offset_of(step):
            return sum(n >> (t + 1) for t in range(step))

        def add(i, step):
            buf, arrivals, c0, width, order, phase, piece = pieces[i]
            count = n >> (step + 1)
            free = [k for k in reversed(range(levels)) if k not in order[: step + 1]]

            def body(j, carry):
                index = list(mine)
                for place, k in enumerate(reversed(free)):
                    index[axis_of(k)] = lax.rem(lax.div(j, 2**place), 2)
                index = tuple(index) + (slice(None), pl.ds(c0, width))
                buf[index] = buf[index] + arrivals[offset_of(step) + j, :, pl.ds(c0, width)]
                return carry

            lax.fori_loop(0, count, body, 0)

        for step in range(levels):
            for i, (buf, arrivals, c0, width, order, phase, piece) in enumerate(pieces):
                if step > 0:
                    pending[i].wait_recv()
                    add(i, step - 1)
                bit = order[step]
                free = [k for k in reversed(range(levels)) if k not in order[: step + 1]]
                count = n >> (step + 1)
                copy = None
                for j in range(count):
                    index = [None] * levels
                    for k in order[:step]:
                        index[axis_of(k)] = my_bit(k)
                    index[axis_of(bit)] = 1 - my_bit(bit)
                    for place, k in enumerate(reversed(free)):
                        index[axis_of(k)] = (j // 2**place) % 2
                    cols = pl.ds(c0, width)
                    copy = pltpu.make_async_remote_copy(
                        src_ref=buf.at[tuple(index) + (slice(None), cols)],
                        dst_ref=arrivals.at[offset_of(step) + j, :, cols],
                        send_sem=send_sem.at[phase, piece, step],
                        recv_sem=recv_sem.at[phase, piece, step],
                        device_id={"dev": partner(bit)},
                        device_id_type=pl.DeviceIdType.MESH,
                    )
                    copy.start()
                span = arrivals.at[pl.ds(offset_of(step), count), :, pl.ds(c0, width)]
                whole = pltpu.make_async_remote_copy(
                    src_ref=span,
                    dst_ref=span,
                    send_sem=send_sem.at[phase, piece, step],
                    recv_sem=recv_sem.at[phase, piece, step],
                    device_id={"dev": partner(bit)},
                    device_id_type=pl.DeviceIdType.MESH,
                )
                pending[i] = whole
                copies.append(whole)
        for i in range(len(pieces)):
            pending[i].wait_recv()
            add(i, levels - 1)
        for copy in copies:
            copy.wait_send()

    gathered[mine + (slice(None), pl.ds(0, hd))] = query_ref[...]
    gathered[mine + (slice(None), pl.ds(hd, fresh_ref.shape[1]))] = fresh_ref[...]
    gate_all[mine] = gates_ref[...]
    pieces = [(gate_all, 0, LANES, orders[0], 1, 0)]
    for i, (c0, width) in enumerate(halves(gathered.shape[-1])):
        pieces.append((gathered, c0, width, orders[i], 0, i))
    gather(pieces)

    owner = owner_ref[...]
    owner_col = owner[:, :1]
    pick = (lax.broadcasted_iota(jnp.int32, (segs, rows), 1) == owner_col).astype(BF16)
    tile = 512

    def pick_queries(j, carry):
        cols = pl.ds(pl.multiple_of(j * tile, tile), tile)
        block = gathered[(slice(None),) * levels + (slice(None), cols)].reshape(rows, tile)
        seg_query[:, cols] = jnp.dot(pick, block, preferred_element_type=F32).astype(BF16)
        return carry

    lax.fori_loop(0, hd // tile, pick_queries, 0)
    loads[0].wait()
    loads[1].wait()

    wide = BLOCK_SEGS * slots
    tall = BLOCK_SEGS * group_size
    row_seg = lax.rem(lax.broadcasted_iota(jnp.int32, (tall, wide), 0), BLOCK_SEGS)
    col_seg = lax.div(lax.broadcasted_iota(jnp.int32, (tall, wide), 1), slots)
    same = row_seg == col_seg
    lane_of = lax.broadcasted_iota(jnp.int32, (BLOCK_SEGS, LANES), 1)
    scale = HEAD_SIZE ** (-0.5)
    stat_max = []
    stat_sum = []
    for b in range(segs // BLOCK_SEGS):
        span = pl.ds(b * BLOCK_SEGS, BLOCK_SEGS)
        bias = bias_ref[b]
        block_max = jnp.zeros((BLOCK_SEGS, LANES), F32)
        block_sum = jnp.zeros((BLOCK_SEGS, LANES), F32)
        for g in range(kv_heads):
            kcols = pl.ds(g * HEAD_SIZE, HEAD_SIZE)
            keys = key_v[span, :, kcols].reshape(wide, HEAD_SIZE)
            values = value_v[span, :, kcols].reshape(wide, HEAD_SIZE)
            stacked = jnp.concatenate(
                [
                    seg_query[span, pl.ds((g * group_size + h) * HEAD_SIZE, HEAD_SIZE)]
                    for h in range(group_size)
                ],
                axis=0,
            )
            scores = lax.dot_general(
                stacked, keys, (((1,), (1,)), ((), ())), preferred_element_type=F32
            )
            scores = jnp.where(same, scores * scale + bias, LOW)
            top = jnp.max(scores, axis=1, keepdims=True)
            prob = jnp.exp(scores - top)
            total = jnp.sum(prob, axis=1, keepdims=True)
            out = jnp.dot(prob.astype(BF16), values, preferred_element_type=F32)
            for h in range(group_size):
                head = g * group_size + h
                lines = slice(h * BLOCK_SEGS, (h + 1) * BLOCK_SEGS)
                seg_out[span, pl.ds(head * HEAD_SIZE, HEAD_SIZE)] = out[lines]
                block_max = jnp.where(lane_of == head, top[lines], block_max)
                block_sum = jnp.where(lane_of == head, total[lines], block_sum)
        stat_max.append(block_max)
        stat_sum.append(block_sum)
    seg_max = jnp.concatenate(stat_max, axis=0)
    seg_sum = jnp.concatenate(stat_sum, axis=0)

    place = lax.broadcasted_iota(jnp.int32, (segs, LANES), 0)

    def scan(value, combine, forward):
        sh = 1
        while sh < segs:
            amount = sh if forward else segs - sh
            moved = pltpu.roll(value, amount, 0)
            near = pltpu.roll(owner, amount, 0)
            inside = (place >= sh) if forward else (place < segs - sh)
            value = jnp.where(inside & (near == owner), combine(value, moved), value)
            sh *= 2
        return value

    row_max = scan(scan(seg_max, jnp.maximum, True), jnp.maximum, False)
    weight = jnp.exp(seg_max - row_max)
    row_sum = scan(seg_sum * weight, jnp.add, True)
    row_sum = jnp.maximum(scan(row_sum, jnp.maximum, False), 1.0)
    row_lse = row_max + jnp.log(row_sum)
    weight = weight / row_sum
    first = (place == 0) | (pltpu.roll(owner, 1, 0) != owner)
    lane = lax.broadcasted_iota(jnp.int32, (segs, LANES), 1)
    stats = jnp.where(lane == HQ, (owner + 1).astype(F32), row_lse)
    stats = jnp.where(first & (lane <= HQ), stats, 0.0)

    to_place = (lax.broadcasted_iota(jnp.int32, (segs, pos_lanes), 1) == owner_col + me).astype(F32)
    stats_t = jnp.dot(
        stats.T, to_place, precision=lax.Precision.HIGHEST, preferred_element_type=F32
    )
    spare = jnp.zeros((8 - per_dev - 1, pos_lanes), F32)
    for d in range(n):
        lse_tab[static_index(d)] = jnp.concatenate(
            [stats_t[d * per_dev : (d + 1) * per_dev], stats_t[HQ : HQ + 1], spare], axis=0
        )
    put = (
        lax.broadcasted_iota(jnp.int32, (pos, segs), 0) == owner_ref[:, :].T[:1, :] + me
    ).astype(BF16)
    for d in range(n):
        scaled = jnp.concatenate(
            [
                (
                    seg_out[:, pl.ds(head * HEAD_SIZE, HEAD_SIZE)] * weight[:, head : head + 1]
                ).astype(BF16)
                for head in range(d * per_dev, (d + 1) * per_dev)
            ],
            axis=1,
        )
        table[static_index(d)] = jnp.dot(put, scaled, preferred_element_type=F32).astype(BF16)

    pieces = [(lse_tab, lse_in, 0, pos_lanes, orders[0], 3, 0)]
    for i, (c0, width) in enumerate(halves(own_cols)):
        pieces.append((table, table_in, c0, width, orders[i], 2, i))
    scatter_sum(pieces)

    my_lse = lse_tab[mine]
    my_table = table[mine]
    row_of = my_lse[per_dev : per_dev + 1, :].astype(jnp.int32) - 1
    hit = lax.broadcasted_iota(jnp.int32, (rows, pos_lanes), 0) == row_of
    heads = []
    full = (slice(None),) * (levels + 1)
    for h in range(per_dev):
        head = me * per_dev + h
        g = lax.div(head, group_size)
        q_cols = pl.ds(pl.multiple_of(head * HEAD_SIZE, HEAD_SIZE), HEAD_SIZE)
        k_cols = pl.ds(pl.multiple_of(hd + g * HEAD_SIZE, HEAD_SIZE), HEAD_SIZE)
        v_cols = pl.ds(pl.multiple_of(hd + (kv_heads + g) * HEAD_SIZE, HEAD_SIZE), HEAD_SIZE)
        q = gathered[full + (q_cols,)].reshape(rows, HEAD_SIZE).astype(F32)
        k = gathered[full + (k_cols,)].reshape(rows, HEAD_SIZE).astype(F32)
        v = gathered[full + (v_cols,)].reshape(rows, HEAD_SIZE).astype(F32)
        own = jnp.sum(q * k, axis=1, keepdims=True) * scale
        lse = jnp.where(hit, my_lse[h : h + 1, :], LOW)
        top = jnp.maximum(jnp.max(lse, axis=1, keepdims=True), own)
        share = jnp.exp(lse - top)
        fresh = jnp.exp(own - top)
        inverse = 1.0 / (jnp.sum(share, axis=1, keepdims=True) + fresh)
        mixed_in = jnp.dot(
            (share * inverse)[:, :pos].astype(BF16),
            my_table[:, h * HEAD_SIZE : (h + 1) * HEAD_SIZE],
            preferred_element_type=F32,
        )
        heads.append((mixed_in + v * (fresh * inverse)).astype(BF16))
    attention = jnp.concatenate(heads, axis=1) if per_dev > 1 else heads[0]

    loads[2].wait()

    def project(j, carry):
        cols = pl.ds(pl.multiple_of(j * tile, tile), tile)
        product = jnp.dot(attention, proj_v[:, cols], preferred_element_type=F32)
        part[full + (cols,)] = product.astype(BF16).reshape((2,) * levels + (row_dev, tile))
        return carry

    lax.fori_loop(0, model // tile, project, 0)
    scatter_sum(
        [
            (part, part_in, c0, width, orders[i], 4, i)
            for i, (c0, width) in enumerate(halves(model))
        ]
    )

    mixed = (hidden_ref[...].astype(F32) + part[mine].astype(F32)).astype(BF16).astype(F32)
    scale_row = lax.rsqrt(jnp.mean(mixed * mixed, axis=1, keepdims=True) + 1e-06)
    normed_all[mine] = (mixed * scale_row * gain_ref[...].astype(F32)).astype(BF16)
    gather(
        [(normed_all, c0, width, orders[i], 5, i) for i, (c0, width) in enumerate(halves(model))]
    )

    all_gates = gate_all[...].reshape(rows, LANES)
    gate_lane = lax.broadcasted_iota(jnp.int32, (rows, LANES), 1)
    gate = jnp.sum(jnp.where(gate_lane == me, all_gates, 0.0), axis=1, keepdims=True)
    loads[3].wait()
    loads[4].wait()
    ff_tile = 256

    def hidden_units(j, carry):
        cols = pl.ds(pl.multiple_of(j * ff_tile, ff_tile), ff_tile)
        tokens = normed_all[...].reshape(rows, model)
        gate_proj = jnp.dot(tokens, wg_v[:, cols], preferred_element_type=F32)
        up_proj = jnp.dot(tokens, wu_v[:, cols], preferred_element_type=F32)
        act_v[:, cols] = (jax.nn.silu(gate_proj) * up_proj).astype(BF16)
        return carry

    lax.fori_loop(0, ff // ff_tile, hidden_units, 0)
    loads[5].wait()

    def down(j, carry):
        cols = pl.ds(pl.multiple_of(j * tile, tile), tile)
        product = jnp.dot(act_v[...], wd_v[:, cols], preferred_element_type=F32)
        part[full + (cols,)] = (
            (product * gate).astype(BF16).reshape((2,) * levels + (row_dev, tile))
        )
        return carry

    lax.fori_loop(0, model // tile, down, 0)
    scatter_sum(
        [
            (part, part_in, c0, width, orders[i], 6, i)
            for i, (c0, width) in enumerate(halves(model))
        ]
    )
    out_ref[...] = (mixed + part[mine].astype(F32)).astype(BF16)


def on_device(
    hidden_in,
    queries,
    fresh_key_value,
    segment_key_cache,
    segment_value_cache,
    segment_owner_row,
    segment_length,
    expert_ids,
    gate_score,
    out_proj,
    norm_gain,
    w_gate,
    w_up,
    w_down,
):
    n = lax.axis_size("dev")
    levels = n.bit_length() - 1
    row_dev, model = hidden_in.shape
    segs, slots, kv_width = segment_key_cache.shape
    kv_heads = kv_width // HEAD_SIZE
    ff = w_gate.shape[2]
    per_dev = HQ // n
    rows = n * row_dev
    pos = rows + n
    pos_lanes = -(-pos // LANES) * LANES
    dims = (n, levels, row_dev, model, ff, segs, slots, kv_heads, per_dev, pos, pos_lanes)
    own_cols = per_dev * HEAD_SIZE
    hd = queries.shape[1]
    fresh = fresh_key_value.reshape(row_dev, 2 * kv_width)
    owner = jnp.broadcast_to(segment_owner_row[:, None], (segs, LANES))
    live = jnp.arange(slots, dtype=jnp.int32)[None, :] < segment_length[:, None]
    bias = jnp.where(live, 0.0, LOW).astype(F32).reshape(
        segs // BLOCK_SEGS, 1, BLOCK_SEGS * slots
    )
    probs = jnp.exp(gate_score.astype(F32) / 4.0)
    probs = probs / jnp.sum(probs, axis=1, keepdims=True)
    chosen = expert_ids[:, :, None] == jnp.arange(LANES, dtype=jnp.int32)[None, None, :]
    gates = jnp.sum(jnp.where(chosen, probs[:, :, None], 0.0), axis=1)
    cube = (2,) * levels
    vmem = pl.BlockSpec(memory_space=pltpu.VMEM)
    hbm = pl.BlockSpec(memory_space=pl.ANY)
    return pl.pallas_call(
        functools.partial(layer_kernel, dims),
        out_shape=jax.ShapeDtypeStruct((row_dev, model), BF16),
        in_specs=[vmem, vmem, vmem, hbm, hbm, vmem, vmem, vmem, hbm, vmem, hbm, hbm, hbm],
        out_specs=vmem,
        scratch_shapes=[
            pltpu.VMEM(segment_key_cache.shape, BF16),
            pltpu.VMEM(segment_value_cache.shape, BF16),
            pltpu.VMEM(out_proj.shape, BF16),
            pltpu.VMEM(w_gate.shape[1:], BF16),
            pltpu.VMEM(w_up.shape[1:], BF16),
            pltpu.VMEM(w_down.shape[1:], BF16),
            pltpu.SemaphoreType.DMA((6,)),
            pltpu.VMEM(cube + (row_dev, hd + 2 * kv_width), BF16),
            pltpu.VMEM(cube + (row_dev, LANES), F32),
            pltpu.VMEM((segs, hd), BF16),
            pltpu.VMEM((segs, hd), F32),
            pltpu.VMEM(cube + (pos, own_cols), BF16),
            pltpu.VMEM((n - 1, pos, own_cols), BF16),
            pltpu.VMEM(cube + (8, pos_lanes), F32),
            pltpu.VMEM((n - 1, 8, pos_lanes), F32),
            pltpu.VMEM(cube + (row_dev, model), BF16),
            pltpu.VMEM((n - 1, row_dev, model), BF16),
            pltpu.VMEM(cube + (row_dev, model), BF16),
            pltpu.VMEM((rows, ff), BF16),
            pltpu.SemaphoreType.DMA((7, 2, levels)),
            pltpu.SemaphoreType.DMA((7, 2, levels)),
        ],
        compiler_params=pltpu.CompilerParams(
            collective_id=0, has_side_effects=True, vmem_limit_bytes=60 * 2**20
        ),
        name="decode_layer",
    )(
        hidden_in,
        queries,
        fresh,
        segment_key_cache,
        segment_value_cache,
        owner,
        bias,
        gates,
        out_proj,
        norm_gain.reshape(1, model),
        w_gate,
        w_up,
        w_down,
    )


def solution(mesh):
    placed = (
        P(("groups", "dev"), None),
        P(("groups", "dev"), None),
        P(("groups", "dev"), None, None),
        P(("groups", "dev"), None, None),
        P(("groups", "dev"), None, None),
        P(("groups", "dev")),
        P(("groups", "dev")),
        P(("groups", "dev"), None),
        P(("groups", "dev"), None),
        P("dev", None),
        P(),
        P("dev", None, None),
        P("dev", None, None),
        P("dev", None, None),
    )
    return jax.shard_map(
        on_device, mesh=mesh, in_specs=placed, out_specs=P(("groups", "dev"), None), check_vma=False
    )
```

```python
import functools

import jax
import jax.numpy as jnp
from jax import lax
from jax.experimental import pallas as pl
from jax.experimental.pallas import tpu as pltpu
from jax.sharding import PartitionSpec as P

HEAD_SIZE = 128
HQ = 32
LANES = 128
BLOCK_SEGS = 16
LOW = -1e30
F32 = jnp.float32
BF16 = jnp.bfloat16


def halves(width, unit):
    half = width // unit // 2 * unit
    return [(0, half), (half, width - half)]


def layer_kernel(
    dims,
    hidden_hbm,
    query_hbm,
    fresh_ref,
    key_hbm,
    value_hbm,
    owner_ref,
    length_ref,
    ids_ref,
    score_ref,
    proj_hbm,
    gain_ref,
    wg_hbm,
    wu_hbm,
    wd_hbm,
    out_ref,
    key_v,
    value_v,
    proj_v,
    wg_v,
    wu_v,
    wd_v,
    hidden_v,
    load_sem,
    gathered,
    gate_all,
    seg_query,
    seg_out,
    table,
    table_sib,
    table_ring,
    lse_tab,
    lse_sib,
    lse_ring,
    part,
    part_sib,
    part_ring,
    normed_all,
    act_v,
    send_sem,
    recv_sem,
):
    n, snake, row_dev, model, ff, segs, slots, kv_heads, per_dev, pos, pos_lanes = dims
    rows = n * row_dev
    group_size = HQ // kv_heads
    hd = HQ * HEAD_SIZE
    kv_width = kv_heads * HEAD_SIZE
    own_cols = per_dev * HEAD_SIZE
    me = lax.axis_index("dev")

    chips = n // 2
    reach = chips // 2
    core = lax.rem(me, 2)
    chip = lax.div(me, 2)
    if snake:
        side = lax.rem(chip, 2)
        along = lax.div(chip, 2)
        spot = along * (1 - side) + (chips - 1 - along) * side
    else:
        spot = chip

    def chip_at(offset):
        p = lax.rem(spot + offset + chips, chips)
        if not snake:
            return p
        back = lax.div(p, chips // 2)
        return (1 - back) * 2 * p + back * (2 * (chips - 1 - p) + 1)

    sibling = chip * 2 + 1 - core
    beside = {d: chip_at(d) * 2 + core for d in (1, -1)}
    offsets = [reach]
    for dist in range(reach - 1, 0, -1):
        offsets += [dist, -dist]
    offsets.append(0)

    def slot_of(offset):
        return offsets.index(reach if offset == -reach else offset)

    def ring_slot(d, step):
        return chips + (0 if d == 1 else reach) + step

    loads = []
    for i, (src, dst) in enumerate(
        [
            (query_hbm, gathered.at[me, :, pl.ds(0, hd)]),
            (key_hbm, key_v),
            (value_hbm, value_v),
            (hidden_hbm, hidden_v),
            (proj_hbm, proj_v),
            (wg_hbm.at[0], wg_v),
            (wu_hbm.at[0], wu_v),
            (wd_hbm.at[0], wd_v),
        ]
    ):
        copy = pltpu.make_async_copy(src, dst, load_sem.at[i])
        copy.start()
        loads.append(copy)

    barrier = pltpu.get_barrier_semaphore()
    for other in (beside[1], beside[-1], sibling):
        pl.semaphore_signal(
            barrier, inc=1, device_id={"dev": other}, device_id_type=pl.DeviceIdType.MESH
        )

    def remote(src, dst, phase, piece, slot, device):
        copy = pltpu.make_async_remote_copy(
            src_ref=src,
            dst_ref=dst,
            send_sem=send_sem.at[phase, piece, slot],
            recv_sem=recv_sem.at[phase, piece, slot],
            device_id={"dev": device},
            device_id_type=pl.DeviceIdType.MESH,
        )
        copy.start()
        return copy

    def gather(phase, pieces):
        copies = []
        ring = {}
        beside_me = []

        def to_sibling(i, offset):
            buf, cut, far = pieces[i]
            ref = buf.at[(chip_at(offset) * 2 + core,) + cut]
            copy = remote(ref, ref, phase, i, slot_of(offset), sibling)
            copies.append(copy)
            beside_me.append(copy)

        for step in range(reach):
            for i, (buf, cut, far) in enumerate(pieces):
                for d in (1, -1):
                    if step > 0:
                        ring[d, step - 1, i].wait_recv()
                    if step == reach - 1 and far != d:
                        continue
                    ref = buf.at[(chip_at(-d * step) * 2 + core,) + cut]
                    copy = remote(ref, ref, phase, i, ring_slot(d, step), beside[d])
                    ring[d, step, i] = copy
                    copies.append(copy)
            for i in range(len(pieces)):
                for offset in (step, -step) if step else (0,):
                    to_sibling(i, offset)
        for i, (buf, cut, far) in enumerate(pieces):
            ring[far, reach - 1, i].wait_recv()
            to_sibling(i, reach)
        for copy in beside_me:
            copy.wait_recv()
        for copy in copies:
            copy.wait_send()

    def scatter_sum(phase, pieces):
        copies = []
        ring = {}
        near = {}
        for offset in offsets:
            for i, (buf, sib, ring_in, cut, far) in enumerate(pieces):
                slot = slot_of(offset)
                copy = remote(
                    buf.at[(chip_at(offset) * 2 + 1 - core,) + cut],
                    sib.at[(slot,) + cut],
                    phase,
                    i,
                    slot,
                    sibling,
                )
                copies.append(copy)
                near[slot, i] = copy
        for step in range(reach):
            for i, (buf, sib, ring_in, cut, far) in enumerate(pieces):
                for d in (1, -1):
                    if step == 0 and far != d:
                        continue
                    offset = d * (reach - step)
                    slot = slot_of(offset)
                    where = (chip_at(offset) * 2 + core,) + cut
                    near[slot, i].wait_recv()
                    total = buf[where].astype(F32) + sib[(slot,) + cut].astype(F32)
                    if (d, step - 1, i) in ring:
                        ring[d, step - 1, i].wait_recv()
                        total = total + ring_in[(0 if d == 1 else 1, step - 1) + cut].astype(F32)
                    buf[where] = total.astype(buf.dtype)
                    copy = remote(
                        buf.at[where],
                        ring_in.at[(0 if d == 1 else 1, step) + cut],
                        phase,
                        i,
                        ring_slot(d, step),
                        beside[d],
                    )
                    ring[d, step, i] = copy
                    copies.append(copy)
        for i, (buf, sib, ring_in, cut, far) in enumerate(pieces):
            slot = slot_of(0)
            near[slot, i].wait_recv()
            total = buf[(me,) + cut].astype(F32) + sib[(slot,) + cut].astype(F32)
            for d in (1, -1):
                ring[d, reach - 1, i].wait_recv()
                total = total + ring_in[(0 if d == 1 else 1, reach - 1) + cut].astype(F32)
            buf[(me,) + cut] = total.astype(buf.dtype)
        for copy in copies:
            copy.wait_send()

    gathered[me, :, pl.ds(hd, kv_width)] = fresh_ref[:, 0, :]
    gathered[me, :, pl.ds(hd + kv_width, kv_width)] = fresh_ref[:, 1, :]
    probs = jnp.exp(score_ref[...].astype(F32) / 4.0)
    probs = probs / jnp.sum(probs, axis=0, keepdims=True)
    expert_of = lax.broadcasted_iota(jnp.int32, (LANES, row_dev), 0)
    gates = jnp.zeros((LANES, row_dev), F32)
    for k in range(ids_ref.shape[0]):
        gates = gates + jnp.where(ids_ref[k : k + 1, :] == expert_of, probs[k : k + 1, :], 0.0)
    gate_all[me] = gates.T
    loads[0].wait()
    pl.semaphore_wait(barrier, 3)
    every = (slice(None), slice(None))
    cuts = [(slice(None), pl.ds(c0, w)) for c0, w in halves(gathered.shape[-1], LANES)]
    gather(0, [(gathered, cuts[0], 1), (gathered, cuts[1], -1), (gate_all, every, 1)])

    owner_line = owner_ref[...]
    owner = jnp.broadcast_to(owner_line, (LANES, segs)).astype(F32).T.astype(jnp.int32)
    owner_col = owner[:, :1]
    blocks = segs // BLOCK_SEGS
    in_block = (
        lax.div(lax.broadcasted_iota(jnp.int32, (blocks, segs), 1), BLOCK_SEGS)
        == lax.broadcasted_iota(jnp.int32, (blocks, segs), 0)
    )
    lengths = jnp.where(in_block, length_ref[...].astype(F32), 0.0).astype(BF16)
    spread_shape = (segs, BLOCK_SEGS * slots)
    spread = (
        lax.rem(lax.broadcasted_iota(jnp.int32, spread_shape, 0), BLOCK_SEGS)
        == lax.div(lax.broadcasted_iota(jnp.int32, spread_shape, 1), slots)
    ).astype(BF16)
    live = jnp.dot(lengths, spread, preferred_element_type=F32)
    slot_id = lax.rem(lax.broadcasted_iota(jnp.int32, live.shape, 1), slots).astype(F32)
    bias_all = jnp.where(slot_id < live, 0.0, LOW)
    pick = (lax.broadcasted_iota(jnp.int32, (segs, rows), 1) == owner_col).astype(BF16)
    tile = 512

    def pick_queries(j, carry):
        cols = pl.ds(pl.multiple_of(j * tile, tile), tile)
        block = gathered[:, :, cols].reshape(rows, tile)
        seg_query[:, cols] = jnp.dot(pick, block, preferred_element_type=F32).astype(BF16)
        return carry

    lax.fori_loop(0, hd // tile, pick_queries, 0)
    loads[1].wait()
    loads[2].wait()

    wide = BLOCK_SEGS * slots
    tall = BLOCK_SEGS * group_size
    row_seg = lax.rem(lax.broadcasted_iota(jnp.int32, (tall, wide), 0), BLOCK_SEGS)
    col_seg = lax.div(lax.broadcasted_iota(jnp.int32, (tall, wide), 1), slots)
    same = row_seg == col_seg
    lane_of = lax.broadcasted_iota(jnp.int32, (BLOCK_SEGS, LANES), 1)
    scale = HEAD_SIZE ** (-0.5)
    stat_max = []
    stat_sum = []
    for b in range(blocks):
        span = pl.ds(b * BLOCK_SEGS, BLOCK_SEGS)
        bias = bias_all[b : b + 1]
        block_max = jnp.zeros((BLOCK_SEGS, LANES), F32)
        block_sum = jnp.zeros((BLOCK_SEGS, LANES), F32)
        for g in range(kv_heads):
            kcols = pl.ds(g * HEAD_SIZE, HEAD_SIZE)
            keys = key_v[span, :, kcols].reshape(wide, HEAD_SIZE)
            values = value_v[span, :, kcols].reshape(wide, HEAD_SIZE)
            stacked = jnp.concatenate(
                [
                    seg_query[span, pl.ds((g * group_size + h) * HEAD_SIZE, HEAD_SIZE)]
                    for h in range(group_size)
                ],
                axis=0,
            )
            scores = lax.dot_general(
                stacked, keys, (((1,), (1,)), ((), ())), preferred_element_type=F32
            )
            scores = jnp.where(same, scores * scale + bias, LOW)
            top = jnp.max(scores, axis=1, keepdims=True)
            prob = jnp.exp(scores - top)
            total = jnp.sum(prob, axis=1, keepdims=True)
            out = jnp.dot(prob.astype(BF16), values, preferred_element_type=F32)
            for h in range(group_size):
                head = g * group_size + h
                lines = slice(h * BLOCK_SEGS, (h + 1) * BLOCK_SEGS)
                seg_out[span, pl.ds(head * HEAD_SIZE, HEAD_SIZE)] = out[lines]
                block_max = jnp.where(lane_of == head, top[lines], block_max)
                block_sum = jnp.where(lane_of == head, total[lines], block_sum)
        stat_max.append(block_max)
        stat_sum.append(block_sum)
    seg_max = jnp.concatenate(stat_max, axis=0)
    seg_sum = jnp.concatenate(stat_sum, axis=0)

    place = lax.broadcasted_iota(jnp.int32, (segs, LANES), 0)

    def scan(value, combine, forward):
        sh = 1
        while sh < segs:
            amount = sh if forward else segs - sh
            moved = pltpu.roll(value, amount, 0)
            near = pltpu.roll(owner, amount, 0)
            inside = (place >= sh) if forward else (place < segs - sh)
            value = jnp.where(inside & (near == owner), combine(value, moved), value)
            sh *= 2
        return value

    row_max = scan(scan(seg_max, jnp.maximum, True), jnp.maximum, False)
    weight = jnp.exp(seg_max - row_max)
    row_sum = scan(seg_sum * weight, jnp.add, True)
    row_sum = jnp.maximum(scan(row_sum, jnp.maximum, False), 1.0)
    row_lse = row_max + jnp.log(row_sum)
    weight = weight / row_sum
    first = (place == 0) | (pltpu.roll(owner, 1, 0) != owner)
    lane = lax.broadcasted_iota(jnp.int32, (segs, LANES), 1)
    stats = jnp.where(lane == HQ, (owner + 1).astype(F32), row_lse)
    stats = jnp.where(first & (lane <= HQ), stats, 0.0)

    to_place = (lax.broadcasted_iota(jnp.int32, (segs, pos_lanes), 1) == owner_col + me).astype(F32)
    stats_t = jnp.dot(
        stats.T, to_place, precision=lax.Precision.HIGHEST, preferred_element_type=F32
    )
    spare = jnp.zeros((8 - per_dev - 1, pos_lanes), F32)
    for d in range(n):
        lse_tab[d] = jnp.concatenate(
            [stats_t[d * per_dev : (d + 1) * per_dev], stats_t[HQ : HQ + 1], spare], axis=0
        )
    put = (
        lax.broadcasted_iota(jnp.int32, (pos, segs), 0) == owner_line + me
    ).astype(BF16)
    for d in range(n):
        scaled = jnp.concatenate(
            [
                (
                    seg_out[:, pl.ds(head * HEAD_SIZE, HEAD_SIZE)] * weight[:, head : head + 1]
                ).astype(BF16)
                for head in range(d * per_dev, (d + 1) * per_dev)
            ],
            axis=1,
        )
        table[d] = jnp.dot(put, scaled, preferred_element_type=F32).astype(BF16)

    cuts = [(pl.ds(r0, c), slice(None)) for r0, c in halves(pos, 16)]
    scatter_sum(
        1,
        [
            (table, table_sib, table_ring, cuts[0], 1),
            (table, table_sib, table_ring, cuts[1], -1),
            (lse_tab, lse_sib, lse_ring, every, 1),
        ],
    )

    my_lse = lse_tab[me]
    my_table = table[me]
    row_of = my_lse[per_dev : per_dev + 1, :].astype(jnp.int32) - 1
    hit = lax.broadcasted_iota(jnp.int32, (rows, pos_lanes), 0) == row_of
    heads = []
    full = (slice(None), slice(None))
    for h in range(per_dev):
        head = me * per_dev + h
        g = lax.div(head, group_size)
        q_cols = pl.ds(pl.multiple_of(head * HEAD_SIZE, HEAD_SIZE), HEAD_SIZE)
        k_cols = pl.ds(pl.multiple_of(hd + g * HEAD_SIZE, HEAD_SIZE), HEAD_SIZE)
        v_cols = pl.ds(pl.multiple_of(hd + (kv_heads + g) * HEAD_SIZE, HEAD_SIZE), HEAD_SIZE)
        q = gathered[full + (q_cols,)].reshape(rows, HEAD_SIZE).astype(F32)
        k = gathered[full + (k_cols,)].reshape(rows, HEAD_SIZE).astype(F32)
        v = gathered[full + (v_cols,)].reshape(rows, HEAD_SIZE).astype(F32)
        own = jnp.sum(q * k, axis=1, keepdims=True) * scale
        lse = jnp.where(hit, my_lse[h : h + 1, :], LOW)
        top = jnp.maximum(jnp.max(lse, axis=1, keepdims=True), own)
        share = jnp.exp(lse - top)
        fresh = jnp.exp(own - top)
        inverse = 1.0 / (jnp.sum(share, axis=1, keepdims=True) + fresh)
        mixed_in = jnp.dot(
            (share * inverse)[:, :pos].astype(BF16),
            my_table[:, h * HEAD_SIZE : (h + 1) * HEAD_SIZE],
            preferred_element_type=F32,
        )
        heads.append((mixed_in + v * (fresh * inverse)).astype(BF16))
    attention = jnp.concatenate(heads, axis=1) if per_dev > 1 else heads[0]

    loads[4].wait()

    def project(j, carry):
        cols = pl.ds(pl.multiple_of(j * tile, tile), tile)
        product = jnp.dot(attention, proj_v[:, cols], preferred_element_type=F32)
        part[full + (cols,)] = product.astype(BF16).reshape(n, row_dev, tile)
        return carry

    lax.fori_loop(0, model // tile, project, 0)
    cuts = [(slice(None), pl.ds(c0, w)) for c0, w in halves(model, LANES)]
    part_pieces = [
        (part, part_sib, part_ring, cuts[0], 1),
        (part, part_sib, part_ring, cuts[1], -1),
    ]
    scatter_sum(2, part_pieces)

    loads[3].wait()
    mixed = (hidden_v[...].astype(F32) + part[me].astype(F32)).astype(BF16).astype(F32)
    scale_row = lax.rsqrt(jnp.mean(mixed * mixed, axis=1, keepdims=True) + 1e-06)
    normed_all[me] = (mixed * scale_row * gain_ref[...].astype(F32).reshape(1, model)).astype(BF16)
    gather(3, [(normed_all, cuts[0], 1), (normed_all, cuts[1], -1)])

    all_gates = gate_all[...].reshape(rows, LANES)
    gate_lane = lax.broadcasted_iota(jnp.int32, (rows, LANES), 1)
    gate = jnp.sum(jnp.where(gate_lane == me, all_gates, 0.0), axis=1, keepdims=True)
    loads[5].wait()
    loads[6].wait()
    ff_tile = 256

    def hidden_units(j, carry):
        cols = pl.ds(pl.multiple_of(j * ff_tile, ff_tile), ff_tile)
        tokens = normed_all[...].reshape(rows, model)
        gate_proj = jnp.dot(tokens, wg_v[:, cols], preferred_element_type=F32)
        up_proj = jnp.dot(tokens, wu_v[:, cols], preferred_element_type=F32)
        act_v[:, cols] = (jax.nn.silu(gate_proj) * up_proj).astype(BF16)
        return carry

    lax.fori_loop(0, ff // ff_tile, hidden_units, 0)
    loads[7].wait()

    def down(j, carry):
        cols = pl.ds(pl.multiple_of(j * tile, tile), tile)
        product = jnp.dot(act_v[...], wd_v[:, cols], preferred_element_type=F32)
        part[full + (cols,)] = (
            (product * gate).astype(BF16).reshape(n, row_dev, tile)
        )
        return carry

    lax.fori_loop(0, model // tile, down, 0)
    scatter_sum(4, part_pieces)
    out_ref[...] = (mixed + part[me].astype(F32)).astype(BF16)


def on_device(
    snake,
    hidden_in,
    queries,
    fresh_key_value,
    segment_key_cache,
    segment_value_cache,
    segment_owner_row,
    segment_length,
    expert_ids,
    gate_score,
    out_proj,
    norm_gain,
    w_gate,
    w_up,
    w_down,
):
    n = lax.axis_size("dev")
    chips = n // 2
    row_dev, model = hidden_in.shape
    segs, slots, kv_width = segment_key_cache.shape
    kv_heads = kv_width // HEAD_SIZE
    ff = w_gate.shape[2]
    per_dev = HQ // n
    rows = n * row_dev
    pos = rows + n
    pos_lanes = -(-pos // LANES) * LANES
    dims = (n, snake, row_dev, model, ff, segs, slots, kv_heads, per_dev, pos, pos_lanes)
    own_cols = per_dev * HEAD_SIZE
    hd = queries.shape[1]
    vmem = pl.BlockSpec(memory_space=pltpu.VMEM)
    hbm = pl.BlockSpec(memory_space=pl.ANY)
    return pl.pallas_call(
        functools.partial(layer_kernel, dims),
        out_shape=jax.ShapeDtypeStruct((row_dev, model), BF16),
        in_specs=[hbm, hbm, vmem, hbm, hbm] + [vmem] * 4 + [hbm, vmem, hbm, hbm, hbm],
        out_specs=vmem,
        scratch_shapes=[
            pltpu.VMEM(segment_key_cache.shape, BF16),
            pltpu.VMEM(segment_value_cache.shape, BF16),
            pltpu.VMEM(out_proj.shape, BF16),
            pltpu.VMEM(w_gate.shape[1:], BF16),
            pltpu.VMEM(w_up.shape[1:], BF16),
            pltpu.VMEM(w_down.shape[1:], BF16),
            pltpu.VMEM((row_dev, model), BF16),
            pltpu.SemaphoreType.DMA((8,)),
            pltpu.VMEM((n, row_dev, hd + 2 * kv_width), BF16),
            pltpu.VMEM((n, row_dev, LANES), F32),
            pltpu.VMEM((segs, hd), BF16),
            pltpu.VMEM((segs, hd), F32),
            pltpu.VMEM((n, pos, own_cols), BF16),
            pltpu.VMEM((chips, pos, own_cols), BF16),
            pltpu.VMEM((2, chips // 2, pos, own_cols), BF16),
            pltpu.VMEM((n, 8, pos_lanes), F32),
            pltpu.VMEM((chips, 8, pos_lanes), F32),
            pltpu.VMEM((2, chips // 2, 8, pos_lanes), F32),
            pltpu.VMEM((n, row_dev, model), BF16),
            pltpu.VMEM((chips, row_dev, model), BF16),
            pltpu.VMEM((2, chips // 2, row_dev, model), BF16),
            pltpu.VMEM((n, row_dev, model), BF16),
            pltpu.VMEM((rows, ff), BF16),
            pltpu.SemaphoreType.DMA((5, 3, 2 * chips)),
            pltpu.SemaphoreType.DMA((5, 3, 2 * chips)),
        ],
        compiler_params=pltpu.CompilerParams(
            collective_id=0, has_side_effects=True, vmem_limit_bytes=60 * 2**20
        ),
        name="decode_layer",
    )(
        hidden_in,
        queries,
        fresh_key_value,
        segment_key_cache,
        segment_value_cache,
        segment_owner_row.reshape(1, segs),
        segment_length.reshape(1, segs),
        expert_ids.T,
        gate_score.T,
        out_proj,
        norm_gain,
        w_gate,
        w_up,
        w_down,
    )


def snake_ring(mesh):
    places = [getattr(d, "coords", None) for d in mesh.devices.reshape(-1, mesh.shape["dev"])[0]]
    if any(p is None for p in places):
        return False
    places = [tuple(p) for p in places[::2]]
    return len(places) > 2 and len({p[1] for p in places}) == 2 and len({p[2] for p in places}) > 1


def solution(mesh):
    placed = (
        P(("groups", "dev"), None),
        P(("groups", "dev"), None),
        P(("groups", "dev"), None, None),
        P(("groups", "dev"), None, None),
        P(("groups", "dev"), None, None),
        P(("groups", "dev")),
        P(("groups", "dev")),
        P(("groups", "dev"), None),
        P(("groups", "dev"), None),
        P("dev", None),
        P(),
        P("dev", None, None),
        P("dev", None, None),
        P("dev", None, None),
    )
    return jax.shard_map(
        functools.partial(on_device, snake_ring(mesh)),
        mesh=mesh,
        in_specs=placed,
        out_specs=P(("groups", "dev"), None),
        check_vma=False,
    )
```

```python
import functools

import jax
import jax.numpy as jnp
from jax import lax
from jax.experimental import pallas as pl
from jax.experimental.pallas import tpu as pltpu
from jax.sharding import PartitionSpec as P

HEAD_SIZE = 128
HQ = 32
LANES = 128
BLOCK_SEGS = 16
LOW = -1e30
F32 = jnp.float32
BF16 = jnp.bfloat16


def halves(width, unit):
    half = width // unit // 2 * unit
    return [(0, half), (half, width - half)]


def layer_kernel(
    dims,
    hidden_hbm,
    query_hbm,
    fresh_ref,
    key_hbm,
    value_hbm,
    owner_ref,
    length_ref,
    ids_ref,
    score_ref,
    proj_hbm,
    gain_ref,
    wg_hbm,
    wu_hbm,
    wd_hbm,
    out_ref,
    key_v,
    value_v,
    proj_v,
    wg_v,
    wu_v,
    wd_v,
    hidden_v,
    load_sem,
    gathered,
    gate_all,
    seg_query,
    seg_out,
    table,
    table_sib,
    table_ring,
    lse_tab,
    lse_sib,
    lse_ring,
    part,
    part_sib,
    part_ring,
    normed_all,
    scale_all,
    gate_acc,
    up_acc,
    act_v,
    send_sem,
    recv_sem,
):
    n, snake, row_dev, model, ff, segs, slots, kv_heads, per_dev, pos, pos_lanes = dims
    rows = n * row_dev
    group_size = HQ // kv_heads
    hd = HQ * HEAD_SIZE
    kv_width = kv_heads * HEAD_SIZE
    own_cols = per_dev * HEAD_SIZE
    me = lax.axis_index("dev")

    chips = n // 2
    reach = chips // 2
    core = lax.rem(me, 2)
    chip = lax.div(me, 2)
    if snake:
        side = lax.rem(chip, 2)
        along = lax.div(chip, 2)
        spot = along * (1 - side) + (chips - 1 - along) * side
    else:
        spot = chip

    def chip_at(offset):
        p = lax.rem(spot + offset + chips, chips)
        if not snake:
            return p
        back = lax.div(p, chips // 2)
        return (1 - back) * 2 * p + back * (2 * (chips - 1 - p) + 1)

    sibling = chip * 2 + 1 - core
    beside = {d: chip_at(d) * 2 + core for d in (1, -1)}
    offsets = [reach]
    for dist in range(reach - 1, 0, -1):
        offsets += [dist, -dist]
    offsets.append(0)

    def slot_of(offset):
        return offsets.index(reach if offset == -reach else offset)

    def ring_slot(d, step):
        return chips + (0 if d == 1 else reach) + step

    loads = []
    for i, (src, dst) in enumerate(
        [
            (query_hbm, gathered.at[me, :, pl.ds(0, hd)]),
            (key_hbm, key_v),
            (value_hbm, value_v),
            (hidden_hbm, hidden_v),
            (proj_hbm, proj_v),
            (wg_hbm.at[0], wg_v),
            (wu_hbm.at[0], wu_v),
            (wd_hbm.at[0], wd_v),
        ]
    ):
        copy = pltpu.make_async_copy(src, dst, load_sem.at[i])
        copy.start()
        loads.append(copy)

    barrier = pltpu.get_barrier_semaphore()
    for other in (beside[1], beside[-1], sibling):
        pl.semaphore_signal(
            barrier, inc=1, device_id={"dev": other}, device_id_type=pl.DeviceIdType.MESH
        )

    def remote(src, dst, phase, piece, slot, device):
        copy = pltpu.make_async_remote_copy(
            src_ref=src,
            dst_ref=dst,
            send_sem=send_sem.at[phase, piece, slot],
            recv_sem=recv_sem.at[phase, piece, slot],
            device_id={"dev": device},
            device_id_type=pl.DeviceIdType.MESH,
        )
        copy.start()
        return copy

    def gather(phase, pieces):
        copies = []
        ring = {}
        beside_me = []

        def to_sibling(piece, offset):
            number, buf, cut, far = piece
            ref = buf.at[(chip_at(offset) * 2 + core,) + cut]
            copy = remote(ref, ref, phase, number, slot_of(offset), sibling)
            copies.append(copy)
            beside_me.append(copy)

        for step in range(reach):
            for number, buf, cut, far in pieces:
                for d in (1, -1):
                    if step > 0:
                        ring[d, step - 1, number].wait_recv()
                    if step == reach - 1 and far != d:
                        continue
                    ref = buf.at[(chip_at(-d * step) * 2 + core,) + cut]
                    copy = remote(ref, ref, phase, number, ring_slot(d, step), beside[d])
                    ring[d, step, number] = copy
                    copies.append(copy)
            for piece in pieces:
                for offset in (step, -step) if step else (0,):
                    to_sibling(piece, offset)
            yield
        for piece in pieces:
            ring[piece[3], reach - 1, piece[0]].wait_recv()
            to_sibling(piece, reach)
        yield
        for copy in beside_me:
            copy.wait_recv()
        for copy in copies:
            copy.wait_send()

    def scatter_sum(phase, pieces):
        copies = []
        ring = {}
        near = {}
        for offset in offsets:
            for number, buf, sib, ring_in, cut, far in pieces:
                slot = slot_of(offset)
                copy = remote(
                    buf.at[(chip_at(offset) * 2 + 1 - core,) + cut],
                    sib.at[(slot,) + cut],
                    phase,
                    number,
                    slot,
                    sibling,
                )
                copies.append(copy)
                near[slot, number] = copy
        yield
        for step in range(reach):
            for number, buf, sib, ring_in, cut, far in pieces:
                for d in (1, -1):
                    if step == 0 and far != d:
                        continue
                    offset = d * (reach - step)
                    slot = slot_of(offset)
                    where = (chip_at(offset) * 2 + core,) + cut
                    near[slot, number].wait_recv()
                    total = buf[where].astype(F32) + sib[(slot,) + cut].astype(F32)
                    if (d, step - 1, number) in ring:
                        ring[d, step - 1, number].wait_recv()
                        total = total + ring_in[(0 if d == 1 else 1, step - 1) + cut].astype(F32)
                    buf[where] = total.astype(buf.dtype)
                    copy = remote(
                        buf.at[where],
                        ring_in.at[(0 if d == 1 else 1, step) + cut],
                        phase,
                        number,
                        ring_slot(d, step),
                        beside[d],
                    )
                    ring[d, step, number] = copy
                    copies.append(copy)
            yield
        for number, buf, sib, ring_in, cut, far in pieces:
            slot = slot_of(0)
            near[slot, number].wait_recv()
            total = buf[(me,) + cut].astype(F32) + sib[(slot,) + cut].astype(F32)
            for d in (1, -1):
                ring[d, reach - 1, number].wait_recv()
                total = total + ring_in[(0 if d == 1 else 1, reach - 1) + cut].astype(F32)
            buf[(me,) + cut] = total.astype(buf.dtype)
        for copy in copies:
            copy.wait_send()

    def drive(streams, lag):
        streams = list(streams)
        active = [True] * len(streams)
        turn = 0
        while any(active):
            for i, stream in enumerate(streams):
                if active[i] and turn >= lag * i:
                    active[i] = next(stream, "end") != "end"
            turn += 1

    gathered[me, :, pl.ds(hd, kv_width)] = fresh_ref[:, 0, :]
    gathered[me, :, pl.ds(hd + kv_width, kv_width)] = fresh_ref[:, 1, :]
    probs = jnp.exp(score_ref[...].astype(F32) / 4.0)
    probs = probs / jnp.sum(probs, axis=0, keepdims=True)
    expert_of = lax.broadcasted_iota(jnp.int32, (LANES, row_dev), 0)
    gates = jnp.zeros((LANES, row_dev), F32)
    for k in range(ids_ref.shape[0]):
        gates = gates + jnp.where(ids_ref[k : k + 1, :] == expert_of, probs[k : k + 1, :], 0.0)
    gate_all[me] = gates.T
    loads[0].wait()
    pl.semaphore_wait(barrier, 3)
    every = (slice(None), slice(None))

    owner_line = owner_ref[...]
    owner = jnp.broadcast_to(owner_line, (LANES, segs)).astype(F32).T.astype(jnp.int32)
    owner_col = owner[:, :1]
    blocks = segs // BLOCK_SEGS
    in_block = (
        lax.div(lax.broadcasted_iota(jnp.int32, (blocks, segs), 1), BLOCK_SEGS)
        == lax.broadcasted_iota(jnp.int32, (blocks, segs), 0)
    )
    lengths = jnp.where(in_block, length_ref[...].astype(F32), 0.0).astype(BF16)
    spread_shape = (segs, BLOCK_SEGS * slots)
    spread = (
        lax.rem(lax.broadcasted_iota(jnp.int32, spread_shape, 0), BLOCK_SEGS)
        == lax.div(lax.broadcasted_iota(jnp.int32, spread_shape, 1), slots)
    ).astype(BF16)
    live = jnp.dot(lengths, spread, preferred_element_type=F32)
    slot_id = lax.rem(lax.broadcasted_iota(jnp.int32, live.shape, 1), slots).astype(F32)
    bias_all = jnp.where(slot_id < live, 0.0, LOW)
    pick = (lax.broadcasted_iota(jnp.int32, (segs, rows), 1) == owner_col).astype(BF16)
    tile = 512

    def pick_queries(j, carry):
        cols = pl.ds(pl.multiple_of(j * tile, tile), tile)
        block = gathered[:, :, cols].reshape(rows, tile)
        seg_query[:, cols] = jnp.dot(pick, block, preferred_element_type=F32).astype(BF16)
        return carry

    wide = BLOCK_SEGS * slots
    tall = BLOCK_SEGS * group_size
    row_seg = lax.rem(lax.broadcasted_iota(jnp.int32, (tall, wide), 0), BLOCK_SEGS)
    col_seg = lax.div(lax.broadcasted_iota(jnp.int32, (tall, wide), 1), slots)
    same = row_seg == col_seg
    lane_of = lax.broadcasted_iota(jnp.int32, (BLOCK_SEGS, LANES), 1)
    scale = HEAD_SIZE ** (-0.5)
    stat_max = [jnp.zeros((BLOCK_SEGS, LANES), F32)] * blocks
    stat_sum = [jnp.zeros((BLOCK_SEGS, LANES), F32)] * blocks

    def attend(b, g):
        span = pl.ds(b * BLOCK_SEGS, BLOCK_SEGS)
        kcols = pl.ds(g * HEAD_SIZE, HEAD_SIZE)
        keys = key_v[span, :, kcols].reshape(wide, HEAD_SIZE)
        values = value_v[span, :, kcols].reshape(wide, HEAD_SIZE)
        stacked = jnp.concatenate(
            [
                seg_query[span, pl.ds((g * group_size + h) * HEAD_SIZE, HEAD_SIZE)]
                for h in range(group_size)
            ],
            axis=0,
        )
        scores = lax.dot_general(
            stacked, keys, (((1,), (1,)), ((), ())), preferred_element_type=F32
        )
        scores = jnp.where(same, scores * scale + bias_all[b : b + 1], LOW)
        top = jnp.max(scores, axis=1, keepdims=True)
        prob = jnp.exp(scores - top)
        total = jnp.sum(prob, axis=1, keepdims=True)
        out = jnp.dot(prob.astype(BF16), values, preferred_element_type=F32)
        for h in range(group_size):
            head = g * group_size + h
            lines = slice(h * BLOCK_SEGS, (h + 1) * BLOCK_SEGS)
            seg_out[span, pl.ds(head * HEAD_SIZE, HEAD_SIZE)] = out[lines]
            stat_max[b] = jnp.where(lane_of == head, top[lines], stat_max[b])
            stat_sum[b] = jnp.where(lane_of == head, total[lines], stat_sum[b])

    group_cols = group_size * HEAD_SIZE

    def query_stream(g):
        start = g * group_cols
        extent = group_cols
        if g == kv_heads - 1:
            extent += 2 * kv_width
        cuts = [
            (slice(None), pl.ds(start + c0, w)) for c0, w in halves(extent, LANES)
        ]
        pieces = [(2 * g, gathered, cuts[0], 1), (2 * g + 1, gathered, cuts[1], -1)]
        if g == kv_heads - 1:
            pieces.append((2 * kv_heads, gate_all, every, 1))
        yield from gather(0, pieces)
        lax.fori_loop(g * group_cols // tile, (g + 1) * group_cols // tile, pick_queries, 0)
        if g == 0:
            loads[1].wait()
            loads[2].wait()
        for b in range(blocks):
            attend(b, g)
            if b % 2:
                yield

    drive([query_stream(g) for g in range(kv_heads)], 2)
    seg_max = jnp.concatenate(stat_max, axis=0)
    seg_sum = jnp.concatenate(stat_sum, axis=0)

    place = lax.broadcasted_iota(jnp.int32, (segs, LANES), 0)

    def scan(value, combine, forward):
        sh = 1
        while sh < segs:
            amount = sh if forward else segs - sh
            moved = pltpu.roll(value, amount, 0)
            near = pltpu.roll(owner, amount, 0)
            inside = (place >= sh) if forward else (place < segs - sh)
            value = jnp.where(inside & (near == owner), combine(value, moved), value)
            sh *= 2
        return value

    row_max = scan(scan(seg_max, jnp.maximum, True), jnp.maximum, False)
    weight = jnp.exp(seg_max - row_max)
    row_sum = scan(seg_sum * weight, jnp.add, True)
    row_sum = jnp.maximum(scan(row_sum, jnp.maximum, False), 1.0)
    row_lse = row_max + jnp.log(row_sum)
    weight = weight / row_sum
    first = (place == 0) | (pltpu.roll(owner, 1, 0) != owner)
    lane = lax.broadcasted_iota(jnp.int32, (segs, LANES), 1)
    stats = jnp.where(lane == HQ, (owner + 1).astype(F32), row_lse)
    stats = jnp.where(first & (lane <= HQ), stats, 0.0)

    to_place = (lax.broadcasted_iota(jnp.int32, (segs, pos_lanes), 1) == owner_col + me).astype(F32)
    stats_t = jnp.dot(
        stats.T, to_place, precision=lax.Precision.HIGHEST, preferred_element_type=F32
    )
    spare = jnp.zeros((8 - per_dev - 1, pos_lanes), F32)
    for d in range(n):
        lse_tab[d] = jnp.concatenate(
            [stats_t[d * per_dev : (d + 1) * per_dev], stats_t[HQ : HQ + 1], spare], axis=0
        )
    put = (
        lax.broadcasted_iota(jnp.int32, (pos, segs), 0) == owner_line + me
    ).astype(BF16)
    weight_of = [weight[:, head : head + 1] for head in range(HQ)]
    table_cuts = halves(pos, 16)

    def fill_table(h):
        for d in range(n):
            head = d * per_dev + h
            scaled = (
                seg_out[:, pl.ds(head * HEAD_SIZE, HEAD_SIZE)] * weight_of[head]
            ).astype(BF16)
            table[d, :, pl.ds(h * HEAD_SIZE, HEAD_SIZE)] = jnp.dot(
                put, scaled, preferred_element_type=F32
            ).astype(BF16)

    heads = [None] * per_dev
    full = (slice(None), slice(None))

    def combine(h):
        my_lse = lse_tab[me]
        my_table = table[me, :, pl.ds(h * HEAD_SIZE, HEAD_SIZE)]
        row_of = my_lse[per_dev : per_dev + 1, :].astype(jnp.int32) - 1
        hit = lax.broadcasted_iota(jnp.int32, (rows, pos_lanes), 0) == row_of
        head = me * per_dev + h
        g = lax.div(head, group_size)
        q_cols = pl.ds(pl.multiple_of(head * HEAD_SIZE, HEAD_SIZE), HEAD_SIZE)
        k_cols = pl.ds(pl.multiple_of(hd + g * HEAD_SIZE, HEAD_SIZE), HEAD_SIZE)
        v_cols = pl.ds(pl.multiple_of(hd + (kv_heads + g) * HEAD_SIZE, HEAD_SIZE), HEAD_SIZE)
        q = gathered[full + (q_cols,)].reshape(rows, HEAD_SIZE).astype(F32)
        k = gathered[full + (k_cols,)].reshape(rows, HEAD_SIZE).astype(F32)
        v = gathered[full + (v_cols,)].reshape(rows, HEAD_SIZE).astype(F32)
        own = jnp.sum(q * k, axis=1, keepdims=True) * scale
        lse = jnp.where(hit, my_lse[h : h + 1, :], LOW)
        top = jnp.maximum(jnp.max(lse, axis=1, keepdims=True), own)
        share = jnp.exp(lse - top)
        fresh = jnp.exp(own - top)
        inverse = 1.0 / (jnp.sum(share, axis=1, keepdims=True) + fresh)
        mixed_in = jnp.dot(
            (share * inverse)[:, :pos].astype(BF16), my_table, preferred_element_type=F32
        )
        heads[h] = (mixed_in + v * (fresh * inverse)).astype(BF16)

    def table_stream(h):
        fill_table(h)
        cols = pl.ds(h * HEAD_SIZE, HEAD_SIZE)
        pieces = [
            (2 * h + i, table, table_sib, table_ring, (pl.ds(r0, c), cols), far)
            for i, ((r0, c), far) in enumerate(zip(table_cuts, (1, -1)))
        ]
        if h == 0:
            pieces.append((2 * per_dev, lse_tab, lse_sib, lse_ring, every, 1))
        yield from scatter_sum(1, pieces)
        combine(h)

    drive([table_stream(h) for h in range(per_dev)], 1)
    attention = jnp.concatenate(heads, axis=1) if per_dev > 1 else heads[0]

    loads[4].wait()

    def project(j, carry):
        cols = pl.ds(pl.multiple_of(j * tile, tile), tile)
        product = jnp.dot(attention, proj_v[:, cols], preferred_element_type=F32)
        part[full + (cols,)] = product.astype(BF16).reshape(n, row_dev, tile)
        return carry

    stream_cols = [(c0, w) for c0, w in halves(model, tile)]

    def part_pieces(i):
        c0, w = stream_cols[i]
        return [
            (2 * i + j, part, part_sib, part_ring, (slice(None), pl.ds(c0 + at, width)), far)
            for j, ((at, width), far) in enumerate(zip(halves(w, LANES), (1, -1)))
        ]

    mixed_of = [None] * len(stream_cols)
    ff_tile = 256

    def middle_stream(i):
        c0, w = stream_cols[i]
        cols = pl.ds(c0, w)
        lax.fori_loop(c0 // tile, (c0 + w) // tile, project, 0)
        yield from scatter_sum(2, part_pieces(i))
        if i == 0:
            loads[3].wait()
        mixed = hidden_v[:, cols].astype(F32) + part[me, :, cols].astype(F32)
        mixed = mixed.astype(BF16).astype(F32)
        mixed_of[i] = mixed
        gain = gain_ref[cols].astype(F32).reshape(1, w)
        normed_all[me, :, cols] = (mixed * gain).astype(BF16)
        pieces = [
            (2 * i + j, normed_all, (slice(None), pl.ds(c0 + at, width)), far)
            for j, ((at, width), far) in enumerate(zip(halves(w, LANES), (1, -1)))
        ]
        if i == len(stream_cols) - 1:
            squares = sum(jnp.sum(m * m, axis=1, keepdims=True) for m in mixed_of)
            scale_all[me] = jnp.broadcast_to(
                lax.rsqrt(squares / model + 1e-06), (row_dev, LANES)
            )
            pieces.append((2 * len(stream_cols), scale_all, every, 1))
        yield from gather(3, pieces)
        if i == 0:
            loads[5].wait()
            loads[6].wait()
        for j in range(ff // ff_tile):
            units = pl.ds(j * ff_tile, ff_tile)
            tokens = normed_all[:, :, cols].reshape(rows, w)
            gate_proj = jnp.dot(tokens, wg_v[cols, units], preferred_element_type=F32)
            up_proj = jnp.dot(tokens, wu_v[cols, units], preferred_element_type=F32)
            if i > 0:
                gate_proj = gate_proj + gate_acc[:, units]
                up_proj = up_proj + up_acc[:, units]
            if i < len(stream_cols) - 1:
                gate_acc[:, units] = gate_proj
                up_acc[:, units] = up_proj
                yield
            else:
                row_scale = scale_all[...].reshape(rows, LANES)[:, :1]
                gate_proj = gate_proj * row_scale
                up_proj = up_proj * row_scale
                act_v[:, units] = (jax.nn.silu(gate_proj) * up_proj).astype(BF16)

    drive([middle_stream(i) for i in range(len(stream_cols))], 2)

    all_gates = gate_all[...].reshape(rows, LANES)
    gate_lane = lax.broadcasted_iota(jnp.int32, (rows, LANES), 1)
    gate = jnp.sum(jnp.where(gate_lane == me, all_gates, 0.0), axis=1, keepdims=True)
    loads[7].wait()

    def down(j, carry):
        cols = pl.ds(pl.multiple_of(j * tile, tile), tile)
        product = jnp.dot(act_v[...], wd_v[:, cols], preferred_element_type=F32)
        part[full + (cols,)] = (
            (product * gate).astype(BF16).reshape(n, row_dev, tile)
        )
        return carry

    def out_stream(i):
        c0, w = stream_cols[i]
        lax.fori_loop(c0 // tile, (c0 + w) // tile, down, 0)
        yield from scatter_sum(4, part_pieces(i))
        cols = pl.ds(c0, w)
        out_ref[:, cols] = (mixed_of[i] + part[me, :, cols].astype(F32)).astype(BF16)

    drive([out_stream(i) for i in range(len(stream_cols))], 1)


def on_device(
    snake,
    hidden_in,
    queries,
    fresh_key_value,
    segment_key_cache,
    segment_value_cache,
    segment_owner_row,
    segment_length,
    expert_ids,
    gate_score,
    out_proj,
    norm_gain,
    w_gate,
    w_up,
    w_down,
):
    n = lax.axis_size("dev")
    chips = n // 2
    row_dev, model = hidden_in.shape
    segs, slots, kv_width = segment_key_cache.shape
    kv_heads = kv_width // HEAD_SIZE
    ff = w_gate.shape[2]
    per_dev = HQ // n
    rows = n * row_dev
    pos = rows + n
    pos_lanes = -(-pos // LANES) * LANES
    dims = (n, snake, row_dev, model, ff, segs, slots, kv_heads, per_dev, pos, pos_lanes)
    own_cols = per_dev * HEAD_SIZE
    hd = queries.shape[1]
    vmem = pl.BlockSpec(memory_space=pltpu.VMEM)
    hbm = pl.BlockSpec(memory_space=pl.ANY)
    return pl.pallas_call(
        functools.partial(layer_kernel, dims),
        out_shape=jax.ShapeDtypeStruct((row_dev, model), BF16),
        in_specs=[hbm, hbm, vmem, hbm, hbm] + [vmem] * 4 + [hbm, vmem, hbm, hbm, hbm],
        out_specs=vmem,
        scratch_shapes=[
            pltpu.VMEM(segment_key_cache.shape, BF16),
            pltpu.VMEM(segment_value_cache.shape, BF16),
            pltpu.VMEM(out_proj.shape, BF16),
            pltpu.VMEM(w_gate.shape[1:], BF16),
            pltpu.VMEM(w_up.shape[1:], BF16),
            pltpu.VMEM(w_down.shape[1:], BF16),
            pltpu.VMEM((row_dev, model), BF16),
            pltpu.SemaphoreType.DMA((8,)),
            pltpu.VMEM((n, row_dev, hd + 2 * kv_width), BF16),
            pltpu.VMEM((n, row_dev, LANES), F32),
            pltpu.VMEM((segs, hd), BF16),
            pltpu.VMEM((segs, hd), F32),
            pltpu.VMEM((n, pos, own_cols), BF16),
            pltpu.VMEM((chips, pos, own_cols), BF16),
            pltpu.VMEM((2, chips // 2, pos, own_cols), BF16),
            pltpu.VMEM((n, 8, pos_lanes), F32),
            pltpu.VMEM((chips, 8, pos_lanes), F32),
            pltpu.VMEM((2, chips // 2, 8, pos_lanes), F32),
            pltpu.VMEM((n, row_dev, model), BF16),
            pltpu.VMEM((chips, row_dev, model), BF16),
            pltpu.VMEM((2, chips // 2, row_dev, model), BF16),
            pltpu.VMEM((n, row_dev, model), BF16),
            pltpu.VMEM((n, row_dev, LANES), F32),
            pltpu.VMEM((rows, ff), F32),
            pltpu.VMEM((rows, ff), F32),
            pltpu.VMEM((rows, ff), BF16),
            pltpu.SemaphoreType.DMA((5, 5, 2 * chips)),
            pltpu.SemaphoreType.DMA((5, 5, 2 * chips)),
        ],
        compiler_params=pltpu.CompilerParams(
            collective_id=0, has_side_effects=True, vmem_limit_bytes=62 * 2**20
        ),
        name="decode_layer",
    )(
        hidden_in,
        queries,
        fresh_key_value,
        segment_key_cache,
        segment_value_cache,
        segment_owner_row.reshape(1, segs),
        segment_length.reshape(1, segs),
        expert_ids.T,
        gate_score.T,
        out_proj,
        norm_gain,
        w_gate,
        w_up,
        w_down,
    )


def snake_ring(mesh):
    places = [getattr(d, "coords", None) for d in mesh.devices.reshape(-1, mesh.shape["dev"])[0]]
    if any(p is None for p in places):
        return False
    places = [tuple(p) for p in places[::2]]
    return len(places) > 2 and len({p[1] for p in places}) == 2 and len({p[2] for p in places}) > 1


def solution(mesh):
    placed = (
        P(("groups", "dev"), None),
        P(("groups", "dev"), None),
        P(("groups", "dev"), None, None),
        P(("groups", "dev"), None, None),
        P(("groups", "dev"), None, None),
        P(("groups", "dev")),
        P(("groups", "dev")),
        P(("groups", "dev"), None),
        P(("groups", "dev"), None),
        P("dev", None),
        P(),
        P("dev", None, None),
        P("dev", None, None),
        P("dev", None, None),
    )
    return jax.shard_map(
        functools.partial(on_device, snake_ring(mesh)),
        mesh=mesh,
        in_specs=placed,
        out_specs=P(("groups", "dev"), None),
        check_vma=False,
    )
```

```python
import functools

import jax
import jax.numpy as jnp
from jax import lax
from jax.experimental import pallas as pl
from jax.experimental.pallas import tpu as pltpu
from jax.sharding import PartitionSpec as P

HEAD_SIZE = 128
HQ = 32
LANES = 128
BLOCK_SEGS = 16
LOW = -1e30
F32 = jnp.float32
BF16 = jnp.bfloat16


def halves(width, unit):
    half = width // unit // 2 * unit
    return [(0, half), (half, width - half)]


def layer_kernel(
    dims,
    hidden_hbm,
    query_hbm,
    fresh_ref,
    key_hbm,
    value_hbm,
    owner_ref,
    length_ref,
    ids_ref,
    score_ref,
    proj_hbm,
    gain_ref,
    wg_hbm,
    wu_hbm,
    wd_hbm,
    out_ref,
    key_v,
    value_v,
    proj_v,
    wg_v,
    wu_v,
    wd_v,
    hidden_v,
    load_sem,
    gathered,
    seg_query,
    seg_out,
    table,
    table_sib,
    table_ring,
    lse_tab,
    lse_sib,
    lse_ring,
    part,
    part_sib,
    part_ring,
    normed_all,
    act_v,
    send_sem,
    recv_sem,
):
    n, snake, row_dev, model, ff, segs, slots, kv_heads, per_dev, pos, pos_lanes = dims
    rows = n * row_dev
    group_size = HQ // kv_heads
    hd = HQ * HEAD_SIZE
    kv_width = kv_heads * HEAD_SIZE
    own_cols = per_dev * HEAD_SIZE
    me = lax.axis_index("dev")

    chips = n // 2
    reach = chips // 2
    core = lax.rem(me, 2)
    chip = lax.div(me, 2)
    if snake:
        side = lax.rem(chip, 2)
        along = lax.div(chip, 2)
        spot = along * (1 - side) + (chips - 1 - along) * side
    else:
        spot = chip

    def chip_at(offset):
        p = lax.rem(spot + offset + chips, chips)
        if not snake:
            return p
        back = lax.div(p, chips // 2)
        return (1 - back) * 2 * p + back * (2 * (chips - 1 - p) + 1)

    sibling = chip * 2 + 1 - core
    beside = {d: chip_at(d) * 2 + core for d in (1, -1)}
    near = list(range(1, reach - 1)) + [-dist for dist in range(reach - 2, 0, -1)]
    far_away = [reach - 1, reach, 1 - reach]
    offsets = [0] + near + far_away
    near_slots = pl.ds(1, len(near))
    far_slots = pl.ds(1 + len(near), len(far_away))
    not_far = pl.ds(0, 1 + len(near))

    def slot_of(offset):
        return offsets.index(reach if offset == -reach else offset)

    def ring_slot(d, step):
        return 4 + (0 if d == 1 else reach) + step

    places = [chip_at(o) * 2 + c for c in (core, 1 - core) for o in offsets]

    def row_ids(shape, axis):
        index = lax.broadcasted_iota(jnp.int32, shape, axis)
        chunk = lax.div(index, row_dev)
        found = jnp.zeros(shape, jnp.int32)
        for s, device in enumerate(places):
            found = jnp.where(chunk == s, device * row_dev, found)
        return found + lax.rem(index, row_dev)

    loads = []
    for i, (src, dst) in enumerate(
        [
            (query_hbm, gathered.at[0, 0, :, pl.ds(0, hd)]),
            (key_hbm, key_v),
            (value_hbm, value_v),
            (hidden_hbm, hidden_v),
            (proj_hbm, proj_v),
            (wg_hbm.at[0], wg_v),
            (wu_hbm.at[0], wu_v),
            (wd_hbm.at[0], wd_v),
        ]
    ):
        copy = pltpu.make_async_copy(src, dst, load_sem.at[i])
        copy.start()
        loads.append(copy)

    barrier = pltpu.get_barrier_semaphore()
    for other in (beside[1], beside[-1], sibling):
        pl.semaphore_signal(
            barrier, inc=1, device_id={"dev": other}, device_id_type=pl.DeviceIdType.MESH
        )

    def remote(src, dst, phase, piece, slot, device):
        copy = pltpu.make_async_remote_copy(
            src_ref=src,
            dst_ref=dst,
            send_sem=send_sem.at[phase, piece, slot],
            recv_sem=recv_sem.at[phase, piece, slot],
            device_id={"dev": device},
            device_id_type=pl.DeviceIdType.MESH,
        )
        copy.start()
        return copy

    def gather(phase, buf, cuts):
        copies = []
        ring = {}
        beside_me = []

        def to_sibling(number, span):
            copy = remote(buf.at[0, span], buf.at[1, span], phase, 0, number, sibling)
            copies.append(copy)
            beside_me.append(copy)

        for step in range(reach):
            for i, cut in enumerate(cuts):
                for d in (1, -1):
                    if step > 0:
                        ring[d, step - 1, i].wait_recv()
                    if step == reach - 1 and d != 1 - 2 * i:
                        continue
                    copy = remote(
                        buf.at[(0, slot_of(-d * step)) + cut],
                        buf.at[(0, slot_of(-d * (step + 1))) + cut],
                        phase,
                        i,
                        ring_slot(d, step),
                        beside[d],
                    )
                    ring[d, step, i] = copy
                    copies.append(copy)
            if step == 0:
                to_sibling(0, pl.ds(0, 1))
            if step == reach - 2:
                to_sibling(1, near_slots)
        for i in range(len(cuts)):
            ring[1 - 2 * i, reach - 1, i].wait_recv()
        to_sibling(2, far_slots)
        for copy in beside_me:
            copy.wait_recv()
        for copy in copies:
            copy.wait_send()

    def scatter_sum(phase, arrays):
        copies = []
        ring = {}
        crossing = {}
        pieces = []
        for a, (buf, sib, ring_in, cuts) in enumerate(arrays):
            for number, span in enumerate((far_slots, not_far)):
                copy = remote(
                    buf.at[1, span], sib.at[span], phase, 2 * a, number, sibling
                )
                copies.append(copy)
                crossing[a, number] = copy
            for i, cut in enumerate(cuts):
                pieces.append((a, buf, sib, ring_in, cut, 2 * a + i, 1 - 2 * i))

        def crossed(a, number):
            if (a, number) in crossing:
                crossing.pop((a, number)).wait_recv()

        for step in range(reach):
            for a, buf, sib, ring_in, cut, number, far in pieces:
                crossed(a, 0 if step < 2 else 1)
                for d in (1, -1):
                    if step == 0 and far != d:
                        continue
                    slot = slot_of(d * (reach - step))
                    where = (0, slot) + cut
                    total = buf[where].astype(F32) + sib[(slot,) + cut].astype(F32)
                    if (d, step - 1, number) in ring:
                        ring[d, step - 1, number].wait_recv()
                        total = total + ring_in[(0 if d == 1 else 1, step - 1) + cut].astype(F32)
                    buf[where] = total.astype(buf.dtype)
                    copy = remote(
                        buf.at[where],
                        ring_in.at[(0 if d == 1 else 1, step) + cut],
                        phase,
                        number,
                        ring_slot(d, step),
                        beside[d],
                    )
                    ring[d, step, number] = copy
                    copies.append(copy)
        for a, buf, sib, ring_in, cut, number, far in pieces:
            total = buf[(0, 0) + cut].astype(F32) + sib[(0,) + cut].astype(F32)
            for d in (1, -1):
                ring[d, reach - 1, number].wait_recv()
                total = total + ring_in[(0 if d == 1 else 1, reach - 1) + cut].astype(F32)
            buf[(0, 0) + cut] = total.astype(buf.dtype)
        for copy in copies:
            copy.wait_send()

    gathered[0, 0, :, pl.ds(hd, kv_width)] = fresh_ref[:, 0, :]
    gathered[0, 0, :, pl.ds(hd + kv_width, kv_width)] = fresh_ref[:, 1, :]
    probs = jnp.exp(score_ref[...].astype(F32) / 4.0)
    probs = probs / jnp.sum(probs, axis=0, keepdims=True)
    expert_of = lax.broadcasted_iota(jnp.int32, (LANES, row_dev), 0)
    gates = jnp.zeros((LANES, row_dev), F32)
    for k in range(ids_ref.shape[0]):
        gates = gates + jnp.where(ids_ref[k : k + 1, :] == expert_of, probs[k : k + 1, :], 0.0)
    gates = gates.T
    rounded = gates.astype(BF16).astype(F32)
    rest = pltpu.roll(gates - rounded, LANES // 2, 1)
    lane_id = lax.broadcasted_iota(jnp.int32, (row_dev, LANES), 1)
    gathered[0, 0, :, pl.ds(hd + 2 * kv_width, LANES)] = jnp.where(
        lane_id < LANES // 2, rounded, rest
    ).astype(BF16)
    loads[0].wait()
    pl.semaphore_wait(barrier, 3)
    gather(0, gathered, [(slice(None), pl.ds(c0, w)) for c0, w in halves(gathered.shape[-1], LANES)])

    owner_line = owner_ref[...]
    owner = jnp.broadcast_to(owner_line, (LANES, segs)).astype(F32).T.astype(jnp.int32)
    owner_col = owner[:, :1]
    blocks = segs // BLOCK_SEGS
    in_block = (
        lax.div(lax.broadcasted_iota(jnp.int32, (blocks, segs), 1), BLOCK_SEGS)
        == lax.broadcasted_iota(jnp.int32, (blocks, segs), 0)
    )
    lengths = jnp.where(in_block, length_ref[...].astype(F32), 0.0).astype(BF16)
    spread_shape = (segs, BLOCK_SEGS * slots)
    spread = (
        lax.rem(lax.broadcasted_iota(jnp.int32, spread_shape, 0), BLOCK_SEGS)
        == lax.div(lax.broadcasted_iota(jnp.int32, spread_shape, 1), slots)
    ).astype(BF16)
    live = jnp.dot(lengths, spread, preferred_element_type=F32)
    slot_id = lax.rem(lax.broadcasted_iota(jnp.int32, live.shape, 1), slots).astype(F32)
    bias_all = jnp.where(slot_id < live, 0.0, LOW)
    pick = (row_ids((segs, rows), 1) == owner_col).astype(BF16)
    tile = 512

    def pick_queries(j, carry):
        cols = pl.ds(pl.multiple_of(j * tile, tile), tile)
        block = gathered[:, :, :, cols].reshape(rows, tile)
        seg_query[:, cols] = jnp.dot(pick, block, preferred_element_type=F32).astype(BF16)
        return carry

    lax.fori_loop(0, hd // tile, pick_queries, 0)
    loads[1].wait()
    loads[2].wait()

    wide = BLOCK_SEGS * slots
    tall = BLOCK_SEGS * group_size
    row_seg = lax.rem(lax.broadcasted_iota(jnp.int32, (tall, wide), 0), BLOCK_SEGS)
    col_seg = lax.div(lax.broadcasted_iota(jnp.int32, (tall, wide), 1), slots)
    same = row_seg == col_seg
    lane_of = lax.broadcasted_iota(jnp.int32, (BLOCK_SEGS, LANES), 1)
    scale = HEAD_SIZE ** (-0.5)
    stat_max = []
    stat_sum = []
    for b in range(blocks):
        span = pl.ds(b * BLOCK_SEGS, BLOCK_SEGS)
        bias = bias_all[b : b + 1]
        block_max = jnp.zeros((BLOCK_SEGS, LANES), F32)
        block_sum = jnp.zeros((BLOCK_SEGS, LANES), F32)
        for g in range(kv_heads):
            kcols = pl.ds(g * HEAD_SIZE, HEAD_SIZE)
            keys = key_v[span, :, kcols].reshape(wide, HEAD_SIZE)
            values = value_v[span, :, kcols].reshape(wide, HEAD_SIZE)
            stacked = jnp.concatenate(
                [
                    seg_query[span, pl.ds((g * group_size + h) * HEAD_SIZE, HEAD_SIZE)]
                    for h in range(group_size)
                ],
                axis=0,
            )
            scores = lax.dot_general(
                stacked, keys, (((1,), (1,)), ((), ())), preferred_element_type=F32
            )
            scores = jnp.where(same, scores * scale + bias, LOW)
            top = jnp.max(scores, axis=1, keepdims=True)
            prob = jnp.exp(scores - top)
            total = jnp.sum(prob, axis=1, keepdims=True)
            out = jnp.dot(prob.astype(BF16), values, preferred_element_type=F32)
            for h in range(group_size):
                head = g * group_size + h
                lines = slice(h * BLOCK_SEGS, (h + 1) * BLOCK_SEGS)
                seg_out[span, pl.ds(head * HEAD_SIZE, HEAD_SIZE)] = out[lines]
                block_max = jnp.where(lane_of == head, top[lines], block_max)
                block_sum = jnp.where(lane_of == head, total[lines], block_sum)
        stat_max.append(block_max)
        stat_sum.append(block_sum)
    seg_max = jnp.concatenate(stat_max, axis=0)
    seg_sum = jnp.concatenate(stat_sum, axis=0)

    place = lax.broadcasted_iota(jnp.int32, (segs, LANES), 0)

    def scan(value, combine, forward):
        sh = 1
        while sh < segs:
            amount = sh if forward else segs - sh
            moved = pltpu.roll(value, amount, 0)
            near = pltpu.roll(owner, amount, 0)
            inside = (place >= sh) if forward else (place < segs - sh)
            value = jnp.where(inside & (near == owner), combine(value, moved), value)
            sh *= 2
        return value

    row_max = scan(scan(seg_max, jnp.maximum, True), jnp.maximum, False)
    weight = jnp.exp(seg_max - row_max)
    row_sum = scan(seg_sum * weight, jnp.add, True)
    row_sum = jnp.maximum(scan(row_sum, jnp.maximum, False), 1.0)
    row_lse = row_max + jnp.log(row_sum)
    weight = weight / row_sum
    first = (place == 0) | (pltpu.roll(owner, 1, 0) != owner)
    lane = lax.broadcasted_iota(jnp.int32, (segs, LANES), 1)
    stats = jnp.where(lane == HQ, (owner + 1).astype(F32), row_lse)
    stats = jnp.where(first & (lane <= HQ), stats, 0.0)

    to_place = (lax.broadcasted_iota(jnp.int32, (segs, pos_lanes), 1) == owner_col + me).astype(F32)
    stats_t = jnp.dot(
        stats.T, to_place, precision=lax.Precision.HIGHEST, preferred_element_type=F32
    )
    stat_id = lax.broadcasted_iota(jnp.int32, (n * 8, LANES), 0)
    stat_chunk, stat_id = lax.div(stat_id, 8), lax.rem(stat_id, 8)
    wanted = jnp.full((n * 8, LANES), -1, jnp.int32)
    for s, device in enumerate(places):
        wanted = jnp.where(stat_chunk == s, device * per_dev + stat_id, wanted)
    wanted = jnp.where(stat_id < per_dev, wanted, jnp.where(stat_id == per_dev, HQ, -1))
    choose = (wanted == lax.broadcasted_iota(jnp.int32, (n * 8, LANES), 1)).astype(F32)
    lse_tab[...] = jnp.dot(
        choose, stats_t, precision=lax.Precision.HIGHEST, preferred_element_type=F32
    ).reshape(lse_tab.shape)
    put = (
        lax.broadcasted_iota(jnp.int32, (pos, segs), 0) == owner_line + me
    ).astype(BF16)
    for head in range(HQ):
        cols = pl.ds(head * HEAD_SIZE, HEAD_SIZE)
        seg_query[:, cols] = (seg_out[:, cols] * weight[:, head : head + 1]).astype(BF16)
    for s, device in enumerate(places):
        cols = pl.ds(pl.multiple_of(device * own_cols, own_cols), own_cols)
        table[s // chips, s % chips] = jnp.dot(
            put, seg_query[:, cols], preferred_element_type=F32
        ).astype(BF16)

    scatter_sum(
        1,
        [
            (lse_tab, lse_sib, lse_ring, [(slice(None), slice(None))]),
            (
                table,
                table_sib,
                table_ring,
                [(pl.ds(r0, c), slice(None)) for r0, c in halves(pos, 16)],
            ),
        ],
    )

    my_lse = lse_tab[0, 0]
    my_table = table[0, 0]
    row_of = my_lse[per_dev : per_dev + 1, :].astype(jnp.int32) - 1
    hit = row_ids((rows, pos_lanes), 0) == row_of
    heads = []
    full = (slice(None), slice(None), slice(None))
    for h in range(per_dev):
        head = me * per_dev + h
        g = lax.div(head, group_size)
        q_cols = pl.ds(pl.multiple_of(head * HEAD_SIZE, HEAD_SIZE), HEAD_SIZE)
        k_cols = pl.ds(pl.multiple_of(hd + g * HEAD_SIZE, HEAD_SIZE), HEAD_SIZE)
        v_cols = pl.ds(pl.multiple_of(hd + (kv_heads + g) * HEAD_SIZE, HEAD_SIZE), HEAD_SIZE)
        q = gathered[full + (q_cols,)].reshape(rows, HEAD_SIZE).astype(F32)
        k = gathered[full + (k_cols,)].reshape(rows, HEAD_SIZE).astype(F32)
        v = gathered[full + (v_cols,)].reshape(rows, HEAD_SIZE).astype(F32)
        own = jnp.sum(q * k, axis=1, keepdims=True) * scale
        lse = jnp.where(hit, my_lse[h : h + 1, :], LOW)
        top = jnp.maximum(jnp.max(lse, axis=1, keepdims=True), own)
        share = jnp.exp(lse - top)
        fresh = jnp.exp(own - top)
        inverse = 1.0 / (jnp.sum(share, axis=1, keepdims=True) + fresh)
        mixed_in = jnp.dot(
            (share * inverse)[:, :pos].astype(BF16),
            my_table[:, h * HEAD_SIZE : (h + 1) * HEAD_SIZE],
            preferred_element_type=F32,
        )
        heads.append((mixed_in + v * (fresh * inverse)).astype(BF16))
    attention = jnp.concatenate(heads, axis=1) if per_dev > 1 else heads[0]

    loads[4].wait()

    def project(j, carry):
        cols = pl.ds(pl.multiple_of(j * tile, tile), tile)
        product = jnp.dot(attention, proj_v[:, cols], preferred_element_type=F32)
        part[full + (cols,)] = product.astype(BF16).reshape(2, chips, row_dev, tile)
        return carry

    lax.fori_loop(0, model // tile, project, 0)
    cuts = [(slice(None), pl.ds(c0, w)) for c0, w in halves(model, LANES)]
    scatter_sum(2, [(part, part_sib, part_ring, cuts)])

    loads[3].wait()
    mixed = (hidden_v[...].astype(F32) + part[0, 0].astype(F32)).astype(BF16).astype(F32)
    scale_row = lax.rsqrt(jnp.mean(mixed * mixed, axis=1, keepdims=True) + 1e-06)
    normed_all[0, 0] = (mixed * scale_row * gain_ref[...].astype(F32).reshape(1, model)).astype(BF16)
    gather(3, normed_all, cuts)

    all_gates = gathered[full + (pl.ds(hd + 2 * kv_width, LANES),)].reshape(rows, LANES).astype(F32)
    gate_lane = lax.rem(lax.broadcasted_iota(jnp.int32, (rows, LANES), 1), LANES // 2)
    gate = jnp.sum(jnp.where(gate_lane == me, all_gates, 0.0), axis=1, keepdims=True)
    loads[5].wait()
    loads[6].wait()
    ff_tile = 256

    def hidden_units(j, carry):
        cols = pl.ds(pl.multiple_of(j * ff_tile, ff_tile), ff_tile)
        tokens = normed_all[...].reshape(rows, model)
        gate_proj = jnp.dot(tokens, wg_v[:, cols], preferred_element_type=F32)
        up_proj = jnp.dot(tokens, wu_v[:, cols], preferred_element_type=F32)
        act_v[:, cols] = (jax.nn.silu(gate_proj) * up_proj).astype(BF16)
        return carry

    lax.fori_loop(0, ff // ff_tile, hidden_units, 0)
    loads[7].wait()

    def down(j, carry):
        cols = pl.ds(pl.multiple_of(j * tile, tile), tile)
        product = jnp.dot(act_v[...], wd_v[:, cols], preferred_element_type=F32)
        part[full + (cols,)] = (
            (product * gate).astype(BF16).reshape(2, chips, row_dev, tile)
        )
        return carry

    lax.fori_loop(0, model // tile, down, 0)
    scatter_sum(4, [(part, part_sib, part_ring, cuts)])
    out_ref[...] = (mixed + part[0, 0].astype(F32)).astype(BF16)


def on_device(
    snake,
    hidden_in,
    queries,
    fresh_key_value,
    segment_key_cache,
    segment_value_cache,
    segment_owner_row,
    segment_length,
    expert_ids,
    gate_score,
    out_proj,
    norm_gain,
    w_gate,
    w_up,
    w_down,
):
    n = lax.axis_size("dev")
    chips = n // 2
    row_dev, model = hidden_in.shape
    segs, slots, kv_width = segment_key_cache.shape
    kv_heads = kv_width // HEAD_SIZE
    ff = w_gate.shape[2]
    per_dev = HQ // n
    rows = n * row_dev
    pos = rows + n
    pos_lanes = -(-pos // LANES) * LANES
    dims = (n, snake, row_dev, model, ff, segs, slots, kv_heads, per_dev, pos, pos_lanes)
    own_cols = per_dev * HEAD_SIZE
    hd = queries.shape[1]
    vmem = pl.BlockSpec(memory_space=pltpu.VMEM)
    hbm = pl.BlockSpec(memory_space=pl.ANY)
    return pl.pallas_call(
        functools.partial(layer_kernel, dims),
        out_shape=jax.ShapeDtypeStruct((row_dev, model), BF16),
        in_specs=[hbm, hbm, vmem, hbm, hbm] + [vmem] * 4 + [hbm, vmem, hbm, hbm, hbm],
        out_specs=vmem,
        scratch_shapes=[
            pltpu.VMEM(segment_key_cache.shape, BF16),
            pltpu.VMEM(segment_value_cache.shape, BF16),
            pltpu.VMEM(out_proj.shape, BF16),
            pltpu.VMEM(w_gate.shape[1:], BF16),
            pltpu.VMEM(w_up.shape[1:], BF16),
            pltpu.VMEM(w_down.shape[1:], BF16),
            pltpu.VMEM((row_dev, model), BF16),
            pltpu.SemaphoreType.DMA((8,)),
            pltpu.VMEM((2, chips, row_dev, hd + 2 * kv_width + LANES), BF16),
            pltpu.VMEM((segs, hd), BF16),
            pltpu.VMEM((segs, hd), F32),
            pltpu.VMEM((2, chips, pos, own_cols), BF16),
            pltpu.VMEM((chips, pos, own_cols), BF16),
            pltpu.VMEM((2, chips // 2, pos, own_cols), BF16),
            pltpu.VMEM((2, chips, 8, pos_lanes), F32),
            pltpu.VMEM((chips, 8, pos_lanes), F32),
            pltpu.VMEM((2, chips // 2, 8, pos_lanes), F32),
            pltpu.VMEM((2, chips, row_dev, model), BF16),
            pltpu.VMEM((chips, row_dev, model), BF16),
            pltpu.VMEM((2, chips // 2, row_dev, model), BF16),
            pltpu.VMEM((2, chips, row_dev, model), BF16),
            pltpu.VMEM((rows, ff), BF16),
            pltpu.SemaphoreType.DMA((5, 4, 4 + chips)),
            pltpu.SemaphoreType.DMA((5, 4, 4 + chips)),
        ],
        compiler_params=pltpu.CompilerParams(
            collective_id=0, has_side_effects=True, vmem_limit_bytes=60 * 2**20
        ),
        name="decode_layer",
    )(
        hidden_in,
        queries,
        fresh_key_value,
        segment_key_cache,
        segment_value_cache,
        segment_owner_row.reshape(1, segs),
        segment_length.reshape(1, segs),
        expert_ids.T,
        gate_score.T,
        out_proj,
        norm_gain,
        w_gate,
        w_up,
        w_down,
    )


def snake_ring(mesh):
    places = [getattr(d, "coords", None) for d in mesh.devices.reshape(-1, mesh.shape["dev"])[0]]
    if any(p is None for p in places):
        return False
    places = [tuple(p) for p in places[::2]]
    return len(places) > 2 and len({p[1] for p in places}) == 2 and len({p[2] for p in places}) > 1


def solution(mesh):
    placed = (
        P(("groups", "dev"), None),
        P(("groups", "dev"), None),
        P(("groups", "dev"), None, None),
        P(("groups", "dev"), None, None),
        P(("groups", "dev"), None, None),
        P(("groups", "dev")),
        P(("groups", "dev")),
        P(("groups", "dev"), None),
        P(("groups", "dev"), None),
        P("dev", None),
        P(),
        P("dev", None, None),
        P("dev", None, None),
        P("dev", None, None),
    )
    return jax.shard_map(
        functools.partial(on_device, snake_ring(mesh)),
        mesh=mesh,
        in_specs=placed,
        out_specs=P(("groups", "dev"), None),
        check_vma=False,
    )
```

```python
import functools

import jax
import jax.numpy as jnp
from jax import lax
from jax.experimental import pallas as pl
from jax.experimental.pallas import tpu as pltpu
from jax.sharding import PartitionSpec as P

HEAD_SIZE = 128
HQ = 32
LANES = 128
BLOCK_SEGS = 16
LOW = -1e30
F32 = jnp.float32
BF16 = jnp.bfloat16


def halves(width, unit):
    half = width // unit // 2 * unit
    return [(0, half), (half, width - half)]


def layer_kernel(
    dims,
    hidden_hbm,
    query_hbm,
    fresh_ref,
    key_hbm,
    value_hbm,
    owner_ref,
    length_ref,
    ids_ref,
    score_ref,
    proj_hbm,
    gain_ref,
    wg_hbm,
    wu_hbm,
    wd_hbm,
    out_ref,
    key_v,
    value_v,
    proj_v,
    wg_v,
    wu_v,
    wd_v,
    hidden_v,
    load_sem,
    gathered,
    seg_query,
    seg_out,
    table,
    table_sib,
    table_ring,
    lse_tab,
    lse_sib,
    lse_ring,
    part,
    part_sib,
    part_ring,
    normed_all,
    act_v,
    send_sem,
    recv_sem,
):
    n, snake, row_dev, model, ff, segs, slots, kv_heads, per_dev, pos, pos_lanes = dims
    rows = n * row_dev
    group_size = HQ // kv_heads
    hd = HQ * HEAD_SIZE
    kv_width = kv_heads * HEAD_SIZE
    own_cols = per_dev * HEAD_SIZE
    me = lax.axis_index("dev")

    chips = n // 2
    reach = chips // 2
    core = lax.rem(me, 2)
    chip = lax.div(me, 2)
    if snake:
        side = lax.rem(chip, 2)
        along = lax.div(chip, 2)
        spot = along * (1 - side) + (chips - 1 - along) * side
    else:
        spot = chip

    def chip_at(offset):
        p = lax.rem(spot + offset + chips, chips)
        if not snake:
            return p
        back = lax.div(p, chips // 2)
        return (1 - back) * 2 * p + back * (2 * (chips - 1 - p) + 1)

    sibling = chip * 2 + 1 - core
    beside = {d: chip_at(d) * 2 + core for d in (1, -1)}
    across = {d: chip_at(d) * 2 + 1 - core for d in (1, -1)}
    near = list(range(1, reach - 1)) + [-dist for dist in range(reach - 2, 0, -1)]
    offsets = [0] + near + [reach - 1, 1 - reach, reach]
    near_slots = pl.ds(1, len(near))
    far_slots = pl.ds(1 + len(near), 2)
    not_far = pl.ds(0, 1 + len(near))

    def slot_of(offset):
        return offsets.index(reach if offset == -reach else offset)

    def ring_slot(d, step):
        return 4 + (0 if d == 1 else reach) + step

    places = [chip_at(o) * 2 + c for c in (core, 1 - core) for o in offsets]

    def row_ids(shape, axis):
        index = lax.broadcasted_iota(jnp.int32, shape, axis)
        chunk = lax.div(index, row_dev)
        found = jnp.zeros(shape, jnp.int32)
        for s, device in enumerate(places):
            found = jnp.where(chunk == s, device * row_dev, found)
        return found + lax.rem(index, row_dev)

    loads = []
    for i, (src, dst) in enumerate(
        [
            (query_hbm, gathered.at[0, 0, :, pl.ds(0, hd)]),
            (key_hbm, key_v),
            (value_hbm, value_v),
            (hidden_hbm, hidden_v),
            (proj_hbm, proj_v),
            (wg_hbm.at[0], wg_v),
            (wu_hbm.at[0], wu_v),
            (wd_hbm.at[0], wd_v),
        ]
    ):
        copy = pltpu.make_async_copy(src, dst, load_sem.at[i])
        if i < 5:
            copy.start()
        loads.append(copy)

    barrier = pltpu.get_barrier_semaphore()
    for other in (beside[1], beside[-1], across[1], across[-1], sibling):
        pl.semaphore_signal(
            barrier, inc=1, device_id={"dev": other}, device_id_type=pl.DeviceIdType.MESH
        )

    def remote(src, dst, phase, piece, slot, device):
        copy = pltpu.make_async_remote_copy(
            src_ref=src,
            dst_ref=dst,
            send_sem=send_sem.at[phase, piece, slot],
            recv_sem=recv_sem.at[phase, piece, slot],
            device_id={"dev": device},
            device_id_type=pl.DeviceIdType.MESH,
        )
        copy.start()
        return copy

    def gather(phase, buf, cuts):
        copies = []
        ring = {}
        beside_me = []

        def to_sibling(number, span):
            copy = remote(buf.at[0, span], buf.at[1, span], phase, 0, number, sibling)
            copies.append(copy)
            beside_me.append(copy)

        for step in range(reach):
            for i, cut in enumerate(cuts):
                for d in (1, -1):
                    if step > 0:
                        ring[d, step - 1, i].wait_recv()
                    if step == reach - 1 and d != 1 - 2 * i:
                        continue
                    copy = remote(
                        buf.at[(0, slot_of(-d * step)) + cut],
                        buf.at[(0, slot_of(-d * (step + 1))) + cut],
                        phase,
                        i,
                        ring_slot(d, step),
                        beside[d],
                    )
                    ring[d, step, i] = copy
                    copies.append(copy)
                    if step == reach - 1:
                        copy = remote(
                            buf.at[(0, slot_of(-d * step)) + cut],
                            buf.at[(1, slot_of(reach)) + cut],
                            phase,
                            i,
                            3,
                            across[d],
                        )
                        copies.append(copy)
                        beside_me.append(copy)
            if step == 0:
                to_sibling(0, pl.ds(0, 1))
            if step == reach - 2:
                to_sibling(1, near_slots)
        to_sibling(2, far_slots)
        for i in range(len(cuts)):
            ring[1 - 2 * i, reach - 1, i].wait_recv()
        for copy in beside_me:
            copy.wait_recv()
        for copy in copies:
            copy.wait_send()

    def scatter_sum(phase, arrays):
        copies = []
        ring = {}
        crossing = {}
        pieces = []
        for a, (buf, sib, ring_in, cuts) in enumerate(arrays):
            for i, cut in enumerate(cuts):
                pieces.append((a, buf, sib, ring_in, cut, 2 * a + i, 1 - 2 * i))
        for a, buf, sib, ring_in, cut, number, far in pieces:
            side = 0 if far == 1 else 1
            src = slot_of(reach)
            ring[far, 0, number] = remote(
                buf.at[(0, src) + cut],
                ring_in.at[(side, 0) + cut],
                phase,
                number,
                ring_slot(far, 0),
                beside[far],
            )
            ring[0, 0, number] = remote(
                buf.at[(1, src) + cut],
                ring_in.at[(side, reach) + cut],
                phase,
                number,
                3,
                across[far],
            )
            copies += [ring[far, 0, number], ring[0, 0, number]]
        for a, (buf, sib, ring_in, cuts) in enumerate(arrays):
            for number, span in enumerate((far_slots, not_far)):
                copy = remote(
                    buf.at[1, span], sib.at[span], phase, 2 * a, number, sibling
                )
                copies.append(copy)
                crossing[a, number] = copy

        def crossed(a, number):
            if (a, number) in crossing:
                crossing.pop((a, number)).wait_recv()

        for step in range(1, reach):
            for a, buf, sib, ring_in, cut, number, far in pieces:
                crossed(a, 0 if step < 2 else 1)
                for d in (1, -1):
                    slot = slot_of(d * (reach - step))
                    where = (0, slot) + cut
                    total = buf[where].astype(F32) + sib[(slot,) + cut].astype(F32)
                    if (d, step - 1, number) in ring:
                        ring[d, step - 1, number].wait_recv()
                        total = total + ring_in[(0 if d == 1 else 1, step - 1) + cut].astype(F32)
                    if step == 1 and d == far:
                        ring[0, 0, number].wait_recv()
                        total = total + ring_in[(0 if d == 1 else 1, reach) + cut].astype(F32)
                    buf[where] = total.astype(buf.dtype)
                    copy = remote(
                        buf.at[where],
                        ring_in.at[(0 if d == 1 else 1, step) + cut],
                        phase,
                        number,
                        ring_slot(d, step),
                        beside[d],
                    )
                    ring[d, step, number] = copy
                    copies.append(copy)
        for a, buf, sib, ring_in, cut, number, far in pieces:
            total = buf[(0, 0) + cut].astype(F32) + sib[(0,) + cut].astype(F32)
            for d in (1, -1):
                ring[d, reach - 1, number].wait_recv()
                total = total + ring_in[(0 if d == 1 else 1, reach - 1) + cut].astype(F32)
            buf[(0, 0) + cut] = total.astype(buf.dtype)
        for copy in copies:
            copy.wait_send()

    gathered[0, 0, :, pl.ds(hd, kv_width)] = fresh_ref[:, 0, :]
    gathered[0, 0, :, pl.ds(hd + kv_width, kv_width)] = fresh_ref[:, 1, :]
    probs = jnp.exp(score_ref[...].astype(F32) / 4.0)
    probs = probs / jnp.sum(probs, axis=0, keepdims=True)
    expert_of = lax.broadcasted_iota(jnp.int32, (LANES, row_dev), 0)
    gates = jnp.zeros((LANES, row_dev), F32)
    for k in range(ids_ref.shape[0]):
        gates = gates + jnp.where(ids_ref[k : k + 1, :] == expert_of, probs[k : k + 1, :], 0.0)
    gates = gates.T
    rounded = gates.astype(BF16).astype(F32)
    rest = pltpu.roll(gates - rounded, LANES // 2, 1)
    lane_id = lax.broadcasted_iota(jnp.int32, (row_dev, LANES), 1)
    gathered[0, 0, :, pl.ds(hd + 2 * kv_width, LANES)] = jnp.where(
        lane_id < LANES // 2, rounded, rest
    ).astype(BF16)
    loads[0].wait()
    pl.semaphore_wait(barrier, 5)
    gather(0, gathered, [(slice(None), pl.ds(c0, w)) for c0, w in halves(gathered.shape[-1], LANES)])
    for copy in loads[5:]:
        copy.start()

    owner_line = owner_ref[...]
    owner = jnp.broadcast_to(owner_line, (LANES, segs)).astype(F32).T.astype(jnp.int32)
    owner_col = owner[:, :1]
    blocks = segs // BLOCK_SEGS
    in_block = (
        lax.div(lax.broadcasted_iota(jnp.int32, (blocks, segs), 1), BLOCK_SEGS)
        == lax.broadcasted_iota(jnp.int32, (blocks, segs), 0)
    )
    lengths = jnp.where(in_block, length_ref[...].astype(F32), 0.0).astype(BF16)
    spread_shape = (segs, BLOCK_SEGS * slots)
    spread = (
        lax.rem(lax.broadcasted_iota(jnp.int32, spread_shape, 0), BLOCK_SEGS)
        == lax.div(lax.broadcasted_iota(jnp.int32, spread_shape, 1), slots)
    ).astype(BF16)
    live = jnp.dot(lengths, spread, preferred_element_type=F32)
    slot_id = lax.rem(lax.broadcasted_iota(jnp.int32, live.shape, 1), slots).astype(F32)
    bias_all = jnp.where(slot_id < live, 0.0, LOW)
    pick = (row_ids((segs, rows), 1) == owner_col).astype(BF16)
    tile = 512

    def pick_queries(j, carry):
        cols = pl.ds(pl.multiple_of(j * tile, tile), tile)
        block = gathered[:, :, :, cols].reshape(rows, tile)
        seg_query[:, cols] = jnp.dot(pick, block, preferred_element_type=F32).astype(BF16)
        return carry

    lax.fori_loop(0, hd // tile, pick_queries, 0)
    loads[1].wait()
    loads[2].wait()

    wide = BLOCK_SEGS * slots
    tall = BLOCK_SEGS * group_size
    row_seg = lax.rem(lax.broadcasted_iota(jnp.int32, (tall, wide), 0), BLOCK_SEGS)
    col_seg = lax.div(lax.broadcasted_iota(jnp.int32, (tall, wide), 1), slots)
    same = row_seg == col_seg
    lane_of = lax.broadcasted_iota(jnp.int32, (BLOCK_SEGS, LANES), 1)
    scale = HEAD_SIZE ** (-0.5)
    stat_max = []
    stat_sum = []
    for b in range(blocks):
        span = pl.ds(b * BLOCK_SEGS, BLOCK_SEGS)
        bias = bias_all[b : b + 1]
        block_max = jnp.zeros((BLOCK_SEGS, LANES), F32)
        block_sum = jnp.zeros((BLOCK_SEGS, LANES), F32)
        for g in range(kv_heads):
            kcols = pl.ds(g * HEAD_SIZE, HEAD_SIZE)
            keys = key_v[span, :, kcols].reshape(wide, HEAD_SIZE)
            values = value_v[span, :, kcols].reshape(wide, HEAD_SIZE)
            stacked = jnp.concatenate(
                [
                    seg_query[span, pl.ds((g * group_size + h) * HEAD_SIZE, HEAD_SIZE)]
                    for h in range(group_size)
                ],
                axis=0,
            )
            scores = lax.dot_general(
                stacked, keys, (((1,), (1,)), ((), ())), preferred_element_type=F32
            )
            scores = jnp.where(same, scores * scale + bias, LOW)
            top = jnp.max(scores, axis=1, keepdims=True)
            prob = jnp.exp(scores - top)
            total = jnp.sum(prob, axis=1, keepdims=True)
            out = jnp.dot(prob.astype(BF16), values, preferred_element_type=F32)
            for h in range(group_size):
                head = g * group_size + h
                lines = slice(h * BLOCK_SEGS, (h + 1) * BLOCK_SEGS)
                seg_out[span, pl.ds(head * HEAD_SIZE, HEAD_SIZE)] = out[lines]
                block_max = jnp.where(lane_of == head, top[lines], block_max)
                block_sum = jnp.where(lane_of == head, total[lines], block_sum)
        stat_max.append(block_max)
        stat_sum.append(block_sum)
    seg_max = jnp.concatenate(stat_max, axis=0)
    seg_sum = jnp.concatenate(stat_sum, axis=0)

    place = lax.broadcasted_iota(jnp.int32, (segs, LANES), 0)

    def scan(value, combine, forward):
        sh = 1
        while sh < segs:
            amount = sh if forward else segs - sh
            moved = pltpu.roll(value, amount, 0)
            near = pltpu.roll(owner, amount, 0)
            inside = (place >= sh) if forward else (place < segs - sh)
            value = jnp.where(inside & (near == owner), combine(value, moved), value)
            sh *= 2
        return value

    row_max = scan(scan(seg_max, jnp.maximum, True), jnp.maximum, False)
    weight = jnp.exp(seg_max - row_max)
    row_sum = scan(seg_sum * weight, jnp.add, True)
    row_sum = jnp.maximum(scan(row_sum, jnp.maximum, False), 1.0)
    row_lse = row_max + jnp.log(row_sum)
    weight = weight / row_sum
    first = (place == 0) | (pltpu.roll(owner, 1, 0) != owner)
    lane = lax.broadcasted_iota(jnp.int32, (segs, LANES), 1)
    stats = jnp.where(lane == HQ, (owner + 1).astype(F32), row_lse)
    stats = jnp.where(first & (lane <= HQ), stats, 0.0)

    to_place = (lax.broadcasted_iota(jnp.int32, (segs, pos_lanes), 1) == owner_col + me).astype(F32)
    stats_t = jnp.dot(
        stats.T, to_place, precision=lax.Precision.HIGHEST, preferred_element_type=F32
    )
    stat_id = lax.broadcasted_iota(jnp.int32, (n * 8, LANES), 0)
    stat_chunk, stat_id = lax.div(stat_id, 8), lax.rem(stat_id, 8)
    wanted = jnp.full((n * 8, LANES), -1, jnp.int32)
    for s, device in enumerate(places):
        wanted = jnp.where(stat_chunk == s, device * per_dev + stat_id, wanted)
    wanted = jnp.where(stat_id < per_dev, wanted, jnp.where(stat_id == per_dev, HQ, -1))
    choose = (wanted == lax.broadcasted_iota(jnp.int32, (n * 8, LANES), 1)).astype(F32)
    lse_tab[...] = jnp.dot(
        choose, stats_t, precision=lax.Precision.HIGHEST, preferred_element_type=F32
    ).reshape(lse_tab.shape)
    put = (
        lax.broadcasted_iota(jnp.int32, (pos, segs), 0) == owner_line + me
    ).astype(BF16)
    for head in range(HQ):
        cols = pl.ds(head * HEAD_SIZE, HEAD_SIZE)
        seg_query[:, cols] = (seg_out[:, cols] * weight[:, head : head + 1]).astype(BF16)
    for s, device in enumerate(places):
        cols = pl.ds(pl.multiple_of(device * own_cols, own_cols), own_cols)
        table[s // chips, s % chips] = jnp.dot(
            put, seg_query[:, cols], preferred_element_type=F32
        ).astype(BF16)

    scatter_sum(
        1,
        [
            (lse_tab, lse_sib, lse_ring, [(slice(None), slice(None))]),
            (
                table,
                table_sib,
                table_ring,
                [(pl.ds(r0, c), slice(None)) for r0, c in halves(pos, 16)],
            ),
        ],
    )

    my_lse = lse_tab[0, 0]
    my_table = table[0, 0]
    row_of = my_lse[per_dev : per_dev + 1, :].astype(jnp.int32) - 1
    hit = row_ids((rows, pos_lanes), 0) == row_of
    heads = []
    full = (slice(None), slice(None), slice(None))
    for h in range(per_dev):
        head = me * per_dev + h
        g = lax.div(head, group_size)
        q_cols = pl.ds(pl.multiple_of(head * HEAD_SIZE, HEAD_SIZE), HEAD_SIZE)
        k_cols = pl.ds(pl.multiple_of(hd + g * HEAD_SIZE, HEAD_SIZE), HEAD_SIZE)
        v_cols = pl.ds(pl.multiple_of(hd + (kv_heads + g) * HEAD_SIZE, HEAD_SIZE), HEAD_SIZE)
        q = gathered[full + (q_cols,)].reshape(rows, HEAD_SIZE).astype(F32)
        k = gathered[full + (k_cols,)].reshape(rows, HEAD_SIZE).astype(F32)
        v = gathered[full + (v_cols,)].reshape(rows, HEAD_SIZE).astype(F32)
        own = jnp.sum(q * k, axis=1, keepdims=True) * scale
        lse = jnp.where(hit, my_lse[h : h + 1, :], LOW)
        top = jnp.maximum(jnp.max(lse, axis=1, keepdims=True), own)
        share = jnp.exp(lse - top)
        fresh = jnp.exp(own - top)
        inverse = 1.0 / (jnp.sum(share, axis=1, keepdims=True) + fresh)
        mixed_in = jnp.dot(
            (share * inverse)[:, :pos].astype(BF16),
            my_table[:, h * HEAD_SIZE : (h + 1) * HEAD_SIZE],
            preferred_element_type=F32,
        )
        heads.append((mixed_in + v * (fresh * inverse)).astype(BF16))
    attention = jnp.concatenate(heads, axis=1) if per_dev > 1 else heads[0]

    loads[4].wait()

    def project(j, carry):
        cols = pl.ds(pl.multiple_of(j * tile, tile), tile)
        product = jnp.dot(attention, proj_v[:, cols], preferred_element_type=F32)
        part[full + (cols,)] = product.astype(BF16).reshape(2, chips, row_dev, tile)
        return carry

    lax.fori_loop(0, model // tile, project, 0)
    cuts = [(slice(None), pl.ds(c0, w)) for c0, w in halves(model, LANES)]
    scatter_sum(2, [(part, part_sib, part_ring, cuts)])

    loads[3].wait()
    mixed = (hidden_v[...].astype(F32) + part[0, 0].astype(F32)).astype(BF16).astype(F32)
    scale_row = lax.rsqrt(jnp.mean(mixed * mixed, axis=1, keepdims=True) + 1e-06)
    normed_all[0, 0] = (mixed * scale_row * gain_ref[...].astype(F32).reshape(1, model)).astype(BF16)
    gather(3, normed_all, cuts)

    all_gates = gathered[full + (pl.ds(hd + 2 * kv_width, LANES),)].reshape(rows, LANES).astype(F32)
    gate_lane = lax.rem(lax.broadcasted_iota(jnp.int32, (rows, LANES), 1), LANES // 2)
    gate = jnp.sum(jnp.where(gate_lane == me, all_gates, 0.0), axis=1, keepdims=True)
    loads[5].wait()
    loads[6].wait()
    ff_tile = 256

    def hidden_units(j, carry):
        cols = pl.ds(pl.multiple_of(j * ff_tile, ff_tile), ff_tile)
        tokens = normed_all[...].reshape(rows, model)
        gate_proj = jnp.dot(tokens, wg_v[:, cols], preferred_element_type=F32)
        up_proj = jnp.dot(tokens, wu_v[:, cols], preferred_element_type=F32)
        act_v[:, cols] = (jax.nn.silu(gate_proj) * up_proj).astype(BF16)
        return carry

    lax.fori_loop(0, ff // ff_tile, hidden_units, 0)
    loads[7].wait()

    def down(j, carry):
        cols = pl.ds(pl.multiple_of(j * tile, tile), tile)
        product = jnp.dot(act_v[...], wd_v[:, cols], preferred_element_type=F32)
        part[full + (cols,)] = (
            (product * gate).astype(BF16).reshape(2, chips, row_dev, tile)
        )
        return carry

    lax.fori_loop(0, model // tile, down, 0)
    scatter_sum(4, [(part, part_sib, part_ring, cuts)])
    out_ref[...] = (mixed + part[0, 0].astype(F32)).astype(BF16)


def on_device(
    snake,
    hidden_in,
    queries,
    fresh_key_value,
    segment_key_cache,
    segment_value_cache,
    segment_owner_row,
    segment_length,
    expert_ids,
    gate_score,
    out_proj,
    norm_gain,
    w_gate,
    w_up,
    w_down,
):
    n = lax.axis_size("dev")
    chips = n // 2
    row_dev, model = hidden_in.shape
    segs, slots, kv_width = segment_key_cache.shape
    kv_heads = kv_width // HEAD_SIZE
    ff = w_gate.shape[2]
    per_dev = HQ // n
    rows = n * row_dev
    pos = rows + n
    pos_lanes = -(-pos // LANES) * LANES
    dims = (n, snake, row_dev, model, ff, segs, slots, kv_heads, per_dev, pos, pos_lanes)
    own_cols = per_dev * HEAD_SIZE
    hd = queries.shape[1]
    vmem = pl.BlockSpec(memory_space=pltpu.VMEM)
    hbm = pl.BlockSpec(memory_space=pl.ANY)
    return pl.pallas_call(
        functools.partial(layer_kernel, dims),
        out_shape=jax.ShapeDtypeStruct((row_dev, model), BF16),
        in_specs=[hbm, hbm, vmem, hbm, hbm] + [vmem] * 4 + [hbm, vmem, hbm, hbm, hbm],
        out_specs=vmem,
        scratch_shapes=[
            pltpu.VMEM(segment_key_cache.shape, BF16),
            pltpu.VMEM(segment_value_cache.shape, BF16),
            pltpu.VMEM(out_proj.shape, BF16),
            pltpu.VMEM(w_gate.shape[1:], BF16),
            pltpu.VMEM(w_up.shape[1:], BF16),
            pltpu.VMEM(w_down.shape[1:], BF16),
            pltpu.VMEM((row_dev, model), BF16),
            pltpu.SemaphoreType.DMA((8,)),
            pltpu.VMEM((2, chips, row_dev, hd + 2 * kv_width + LANES), BF16),
            pltpu.VMEM((segs, hd), BF16),
            pltpu.VMEM((segs, hd), F32),
            pltpu.VMEM((2, chips, pos, own_cols), BF16),
            pltpu.VMEM((chips, pos, own_cols), BF16),
            pltpu.VMEM((2, chips // 2 + 1, pos, own_cols), BF16),
            pltpu.VMEM((2, chips, 8, pos_lanes), F32),
            pltpu.VMEM((chips, 8, pos_lanes), F32),
            pltpu.VMEM((2, chips // 2 + 1, 8, pos_lanes), F32),
            pltpu.VMEM((2, chips, row_dev, model), BF16),
            pltpu.VMEM((chips, row_dev, model), BF16),
            pltpu.VMEM((2, chips // 2 + 1, row_dev, model), BF16),
            pltpu.VMEM((2, chips, row_dev, model), BF16),
            pltpu.VMEM((rows, ff), BF16),
            pltpu.SemaphoreType.DMA((5, 4, 4 + chips)),
            pltpu.SemaphoreType.DMA((5, 4, 4 + chips)),
        ],
        compiler_params=pltpu.CompilerParams(
            collective_id=0, has_side_effects=True, vmem_limit_bytes=60 * 2**20
        ),
        name="decode_layer",
    )(
        hidden_in,
        queries,
        fresh_key_value,
        segment_key_cache,
        segment_value_cache,
        segment_owner_row.reshape(1, segs),
        segment_length.reshape(1, segs),
        expert_ids.T,
        gate_score.T,
        out_proj,
        norm_gain,
        w_gate,
        w_up,
        w_down,
    )


def snake_ring(mesh):
    places = [getattr(d, "coords", None) for d in mesh.devices.reshape(-1, mesh.shape["dev"])[0]]
    if any(p is None for p in places):
        return False
    places = [tuple(p) for p in places[::2]]
    return len(places) > 2 and len({p[1] for p in places}) == 2 and len({p[2] for p in places}) > 1


def solution(mesh):
    placed = (
        P(("groups", "dev"), None),
        P(("groups", "dev"), None),
        P(("groups", "dev"), None, None),
        P(("groups", "dev"), None, None),
        P(("groups", "dev"), None, None),
        P(("groups", "dev")),
        P(("groups", "dev")),
        P(("groups", "dev"), None),
        P(("groups", "dev"), None),
        P("dev", None),
        P(),
        P("dev", None, None),
        P("dev", None, None),
        P("dev", None, None),
    )
    return jax.shard_map(
        functools.partial(on_device, snake_ring(mesh)),
        mesh=mesh,
        in_specs=placed,
        out_specs=P(("groups", "dev"), None),
        check_vma=False,
    )
```

```python
import functools

import jax
import jax.numpy as jnp
from jax import lax
from jax.experimental import pallas as pl
from jax.experimental.pallas import tpu as pltpu
from jax.sharding import PartitionSpec as P

HEAD_SIZE = 128
HQ = 32
LANES = 128
BLOCK_SEGS = 16
LOW = -1e30
F32 = jnp.float32
BF16 = jnp.bfloat16


def halves(width, unit):
    half = width // unit // 2 * unit
    return [(0, half), (half, width - half)]


def layer_kernel(
    dims,
    hidden_hbm,
    query_hbm,
    fresh_ref,
    key_hbm,
    value_hbm,
    owner_ref,
    length_ref,
    ids_ref,
    score_ref,
    proj_hbm,
    gain_ref,
    wg_hbm,
    wu_hbm,
    wd_hbm,
    out_ref,
    key_v,
    value_v,
    proj_v,
    wg_v,
    wu_v,
    wd_v,
    hidden_v,
    load_sem,
    gathered,
    seg_query,
    seg_out,
    table,
    table_sib,
    table_ring,
    lse_tab,
    lse_sib,
    lse_ring,
    part,
    part_sib,
    part_ring,
    normed_all,
    act_v,
    send_sem,
    recv_sem,
):
    n, snake, row_dev, model, ff, segs, slots, kv_heads, per_dev, pos, pos_lanes = dims
    rows = n * row_dev
    group_size = HQ // kv_heads
    hd = HQ * HEAD_SIZE
    kv_width = kv_heads * HEAD_SIZE
    own_cols = per_dev * HEAD_SIZE
    me = lax.axis_index("dev")

    chips = n // 2
    reach = chips // 2
    core = lax.rem(me, 2)
    chip = lax.div(me, 2)
    if snake:
        side = lax.rem(chip, 2)
        along = lax.div(chip, 2)
        spot = along * (1 - side) + (chips - 1 - along) * side
    else:
        spot = chip

    def chip_at(offset):
        p = lax.rem(spot + offset + chips, chips)
        if not snake:
            return p
        back = lax.div(p, chips // 2)
        return (1 - back) * 2 * p + back * (2 * (chips - 1 - p) + 1)

    sibling = chip * 2 + 1 - core
    beside = {d: chip_at(d) * 2 + core for d in (1, -1)}
    across = {d: chip_at(d) * 2 + 1 - core for d in (1, -1)}
    near = list(range(1, reach - 1)) + [-dist for dist in range(reach - 2, 0, -1)]
    offsets = [0] + near + [reach - 1, 1 - reach, reach]
    near_slots = pl.ds(1, len(near))
    far_slots = pl.ds(1 + len(near), 2)
    not_far = pl.ds(0, 1 + len(near))

    def slot_of(offset):
        return offsets.index(reach if offset == -reach else offset)

    def ring_slot(d, step):
        return 4 + (0 if d == 1 else reach) + step

    places = [chip_at(o) * 2 + c for c in (core, 1 - core) for o in offsets]

    def row_ids(shape, axis):
        index = lax.broadcasted_iota(jnp.int32, shape, axis)
        chunk = lax.div(index, row_dev)
        found = jnp.zeros(shape, jnp.int32)
        for s, device in enumerate(places):
            found = jnp.where(chunk == s, device * row_dev, found)
        return found + lax.rem(index, row_dev)

    loads = []
    for i, (src, dst) in enumerate(
        [
            (query_hbm, gathered.at[0, 0, :, pl.ds(0, hd)]),
            (key_hbm, key_v),
            (value_hbm, value_v),
            (hidden_hbm, hidden_v),
            (proj_hbm, proj_v),
            (wg_hbm.at[0], wg_v),
            (wu_hbm.at[0], wu_v),
            (wd_hbm.at[0], wd_v),
        ]
    ):
        copy = pltpu.make_async_copy(src, dst, load_sem.at[i])
        if i < 5:
            copy.start()
        loads.append(copy)

    barrier = pltpu.get_barrier_semaphore()
    for other in (beside[1], beside[-1], across[1], across[-1], sibling):
        pl.semaphore_signal(
            barrier, inc=1, device_id={"dev": other}, device_id_type=pl.DeviceIdType.MESH
        )

    def remote(src, dst, phase, piece, slot, device):
        copy = pltpu.make_async_remote_copy(
            src_ref=src,
            dst_ref=dst,
            send_sem=send_sem.at[phase, piece, slot],
            recv_sem=recv_sem.at[phase, piece, slot],
            device_id={"dev": device},
            device_id_type=pl.DeviceIdType.MESH,
        )
        copy.start()
        return copy

    def gather(phase, buf, cuts):
        copies = []
        ring = {}
        beside_me = []

        def to_sibling(number, span):
            copy = remote(buf.at[0, span], buf.at[1, span], phase, 0, number, sibling)
            copies.append(copy)
            beside_me.append(copy)

        for step in range(reach):
            for i, cut in enumerate(cuts):
                for d in (1, -1):
                    if step > 0:
                        ring[d, step - 1, i].wait_recv()
                    if step == reach - 1 and d != 1 - 2 * i:
                        continue
                    copy = remote(
                        buf.at[(0, slot_of(-d * step)) + cut],
                        buf.at[(0, slot_of(-d * (step + 1))) + cut],
                        phase,
                        i,
                        ring_slot(d, step),
                        beside[d],
                    )
                    ring[d, step, i] = copy
                    copies.append(copy)
                    if step == reach - 1:
                        copy = remote(
                            buf.at[(0, slot_of(-d * step)) + cut],
                            buf.at[(1, slot_of(reach)) + cut],
                            phase,
                            i,
                            3,
                            across[d],
                        )
                        copies.append(copy)
                        beside_me.append(copy)
            if step == 0:
                to_sibling(0, pl.ds(0, 1))
            if step == reach - 2:
                to_sibling(1, near_slots)
        to_sibling(2, far_slots)
        for i in range(len(cuts)):
            ring[1 - 2 * i, reach - 1, i].wait_recv()
        for copy in beside_me:
            copy.wait_recv()
        for copy in copies:
            copy.wait_send()

    def scatter_sum(phase, arrays, prepare=None):
        copies = []
        ring = {}
        crossing = {}
        pieces = []
        for a, (buf, sib, ring_in, cuts) in enumerate(arrays):
            for i, cut in enumerate(cuts):
                pieces.append((a, buf, sib, ring_in, cut, 2 * a + i, 1 - 2 * i))
        for a, buf, sib, ring_in, cut, number, far in pieces:
            if prepare is not None:
                prepare(number)
            side = 0 if far == 1 else 1
            src = slot_of(reach)
            ring[far, 0, number] = remote(
                buf.at[(0, src) + cut],
                ring_in.at[(side, 0) + cut],
                phase,
                number,
                ring_slot(far, 0),
                beside[far],
            )
            ring[0, 0, number] = remote(
                buf.at[(1, src) + cut],
                ring_in.at[(side, reach) + cut],
                phase,
                number,
                3,
                across[far],
            )
            copies += [ring[far, 0, number], ring[0, 0, number]]
            for part_of, span in enumerate((far_slots, not_far)):
                where = (span,) + cut
                copy = remote(
                    buf.at[(1,) + where], sib.at[where], phase, number, part_of, sibling
                )
                copies.append(copy)
                crossing[number, part_of] = copy

        def crossed(number, part_of):
            if (number, part_of) in crossing:
                crossing.pop((number, part_of)).wait_recv()

        for step in range(1, reach):
            for a, buf, sib, ring_in, cut, number, far in pieces:
                crossed(number, 0 if step < 2 else 1)
                for d in (1, -1):
                    slot = slot_of(d * (reach - step))
                    where = (0, slot) + cut
                    total = buf[where].astype(F32) + sib[(slot,) + cut].astype(F32)
                    if (d, step - 1, number) in ring:
                        ring[d, step - 1, number].wait_recv()
                        total = total + ring_in[(0 if d == 1 else 1, step - 1) + cut].astype(F32)
                    if step == 1 and d == far:
                        ring[0, 0, number].wait_recv()
                        total = total + ring_in[(0 if d == 1 else 1, reach) + cut].astype(F32)
                    buf[where] = total.astype(buf.dtype)
                    copy = remote(
                        buf.at[where],
                        ring_in.at[(0 if d == 1 else 1, step) + cut],
                        phase,
                        number,
                        ring_slot(d, step),
                        beside[d],
                    )
                    ring[d, step, number] = copy
                    copies.append(copy)
        for a, buf, sib, ring_in, cut, number, far in pieces:
            total = buf[(0, 0) + cut].astype(F32) + sib[(0,) + cut].astype(F32)
            for d in (1, -1):
                ring[d, reach - 1, number].wait_recv()
                total = total + ring_in[(0 if d == 1 else 1, reach - 1) + cut].astype(F32)
            buf[(0, 0) + cut] = total.astype(buf.dtype)
        for copy in copies:
            copy.wait_send()

    gathered[0, 0, :, pl.ds(hd, kv_width)] = fresh_ref[:, 0, :]
    gathered[0, 0, :, pl.ds(hd + kv_width, kv_width)] = fresh_ref[:, 1, :]
    probs = jnp.exp(score_ref[...].astype(F32) / 4.0)
    probs = probs / jnp.sum(probs, axis=0, keepdims=True)
    expert_of = lax.broadcasted_iota(jnp.int32, (LANES, row_dev), 0)
    gates = jnp.zeros((LANES, row_dev), F32)
    for k in range(ids_ref.shape[0]):
        gates = gates + jnp.where(ids_ref[k : k + 1, :] == expert_of, probs[k : k + 1, :], 0.0)
    gates = gates.T
    rounded = gates.astype(BF16).astype(F32)
    rest = pltpu.roll(gates - rounded, LANES // 2, 1)
    lane_id = lax.broadcasted_iota(jnp.int32, (row_dev, LANES), 1)
    gathered[0, 0, :, pl.ds(hd + 2 * kv_width, LANES)] = jnp.where(
        lane_id < LANES // 2, rounded, rest
    ).astype(BF16)
    loads[0].wait()
    pl.semaphore_wait(barrier, 5)
    gather(0, gathered, [(slice(None), pl.ds(c0, w)) for c0, w in halves(gathered.shape[-1], LANES)])
    for copy in loads[5:]:
        copy.start()

    owner_line = owner_ref[...]
    owner = jnp.broadcast_to(owner_line, (LANES, segs)).astype(F32).T.astype(jnp.int32)
    owner_col = owner[:, :1]
    blocks = segs // BLOCK_SEGS
    in_block = (
        lax.div(lax.broadcasted_iota(jnp.int32, (blocks, segs), 1), BLOCK_SEGS)
        == lax.broadcasted_iota(jnp.int32, (blocks, segs), 0)
    )
    lengths = jnp.where(in_block, length_ref[...].astype(F32), 0.0).astype(BF16)
    spread_shape = (segs, BLOCK_SEGS * slots)
    spread = (
        lax.rem(lax.broadcasted_iota(jnp.int32, spread_shape, 0), BLOCK_SEGS)
        == lax.div(lax.broadcasted_iota(jnp.int32, spread_shape, 1), slots)
    ).astype(BF16)
    live = jnp.dot(lengths, spread, preferred_element_type=F32)
    slot_id = lax.rem(lax.broadcasted_iota(jnp.int32, live.shape, 1), slots).astype(F32)
    bias_all = jnp.where(slot_id < live, 0.0, LOW)
    pick = (row_ids((segs, rows), 1) == owner_col).astype(BF16)
    tile = 512

    def pick_queries(j, carry):
        cols = pl.ds(pl.multiple_of(j * tile, tile), tile)
        block = gathered[:, :, :, cols].reshape(rows, tile)
        seg_query[:, cols] = jnp.dot(pick, block, preferred_element_type=F32).astype(BF16)
        return carry

    lax.fori_loop(0, hd // tile, pick_queries, 0)
    loads[1].wait()
    loads[2].wait()

    wide = BLOCK_SEGS * slots
    tall = BLOCK_SEGS * group_size
    row_seg = lax.rem(lax.broadcasted_iota(jnp.int32, (tall, wide), 0), BLOCK_SEGS)
    col_seg = lax.div(lax.broadcasted_iota(jnp.int32, (tall, wide), 1), slots)
    same = row_seg == col_seg
    lane_of = lax.broadcasted_iota(jnp.int32, (BLOCK_SEGS, LANES), 1)
    scale = HEAD_SIZE ** (-0.5)
    stat_max = []
    stat_sum = []
    for b in range(blocks):
        span = pl.ds(b * BLOCK_SEGS, BLOCK_SEGS)
        bias = bias_all[b : b + 1]
        block_max = jnp.zeros((BLOCK_SEGS, LANES), F32)
        block_sum = jnp.zeros((BLOCK_SEGS, LANES), F32)
        for g in range(kv_heads):
            kcols = pl.ds(g * HEAD_SIZE, HEAD_SIZE)
            keys = key_v[span, :, kcols].reshape(wide, HEAD_SIZE)
            values = value_v[span, :, kcols].reshape(wide, HEAD_SIZE)
            stacked = jnp.concatenate(
                [
                    seg_query[span, pl.ds((g * group_size + h) * HEAD_SIZE, HEAD_SIZE)]
                    for h in range(group_size)
                ],
                axis=0,
            )
            scores = lax.dot_general(
                stacked, keys, (((1,), (1,)), ((), ())), preferred_element_type=F32
            )
            scores = jnp.where(same, scores * scale + bias, LOW)
            top = jnp.max(scores, axis=1, keepdims=True)
            prob = jnp.exp(scores - top)
            total = jnp.sum(prob, axis=1, keepdims=True)
            out = jnp.dot(prob.astype(BF16), values, preferred_element_type=F32)
            for h in range(group_size):
                head = g * group_size + h
                lines = slice(h * BLOCK_SEGS, (h + 1) * BLOCK_SEGS)
                seg_out[span, pl.ds(head * HEAD_SIZE, HEAD_SIZE)] = out[lines]
                block_max = jnp.where(lane_of == head, top[lines], block_max)
                block_sum = jnp.where(lane_of == head, total[lines], block_sum)
        stat_max.append(block_max)
        stat_sum.append(block_sum)
    seg_max = jnp.concatenate(stat_max, axis=0)
    seg_sum = jnp.concatenate(stat_sum, axis=0)

    place = lax.broadcasted_iota(jnp.int32, (segs, LANES), 0)

    def scan(value, combine, forward):
        sh = 1
        while sh < segs:
            amount = sh if forward else segs - sh
            moved = pltpu.roll(value, amount, 0)
            near = pltpu.roll(owner, amount, 0)
            inside = (place >= sh) if forward else (place < segs - sh)
            value = jnp.where(inside & (near == owner), combine(value, moved), value)
            sh *= 2
        return value

    row_max = scan(scan(seg_max, jnp.maximum, True), jnp.maximum, False)
    weight = jnp.exp(seg_max - row_max)
    row_sum = scan(seg_sum * weight, jnp.add, True)
    row_sum = jnp.maximum(scan(row_sum, jnp.maximum, False), 1.0)
    row_lse = row_max + jnp.log(row_sum)
    weight = weight / row_sum
    first = (place == 0) | (pltpu.roll(owner, 1, 0) != owner)
    lane = lax.broadcasted_iota(jnp.int32, (segs, LANES), 1)
    stats = jnp.where(lane == HQ, (owner + 1).astype(F32), row_lse)
    stats = jnp.where(first & (lane <= HQ), stats, 0.0)

    to_place = (lax.broadcasted_iota(jnp.int32, (segs, pos_lanes), 1) == owner_col + me).astype(F32)
    stats_t = jnp.dot(
        stats.T, to_place, precision=lax.Precision.HIGHEST, preferred_element_type=F32
    )
    stat_id = lax.broadcasted_iota(jnp.int32, (n * 8, LANES), 0)
    stat_chunk, stat_id = lax.div(stat_id, 8), lax.rem(stat_id, 8)
    wanted = jnp.full((n * 8, LANES), -1, jnp.int32)
    for s, device in enumerate(places):
        wanted = jnp.where(stat_chunk == s, device * per_dev + stat_id, wanted)
    wanted = jnp.where(stat_id < per_dev, wanted, jnp.where(stat_id == per_dev, HQ, -1))
    choose = (wanted == lax.broadcasted_iota(jnp.int32, (n * 8, LANES), 1)).astype(F32)
    lse_tab[...] = jnp.dot(
        choose, stats_t, precision=lax.Precision.HIGHEST, preferred_element_type=F32
    ).reshape(lse_tab.shape)
    put = (
        lax.broadcasted_iota(jnp.int32, (pos, segs), 0) == owner_line + me
    ).astype(BF16)
    for head in range(HQ):
        cols = pl.ds(head * HEAD_SIZE, HEAD_SIZE)
        seg_query[:, cols] = (seg_out[:, cols] * weight[:, head : head + 1]).astype(BF16)
    for s, device in enumerate(places):
        cols = pl.ds(pl.multiple_of(device * own_cols, own_cols), own_cols)
        table[s // chips, s % chips] = jnp.dot(
            put, seg_query[:, cols], preferred_element_type=F32
        ).astype(BF16)

    scatter_sum(
        1,
        [
            (lse_tab, lse_sib, lse_ring, [(slice(None), slice(None))]),
            (
                table,
                table_sib,
                table_ring,
                [(pl.ds(r0, c), slice(None)) for r0, c in halves(pos, 16)],
            ),
        ],
    )

    my_lse = lse_tab[0, 0]
    my_table = table[0, 0]
    row_of = my_lse[per_dev : per_dev + 1, :].astype(jnp.int32) - 1
    hit = row_ids((rows, pos_lanes), 0) == row_of
    heads = []
    full = (slice(None), slice(None), slice(None))
    for h in range(per_dev):
        head = me * per_dev + h
        g = lax.div(head, group_size)
        q_cols = pl.ds(pl.multiple_of(head * HEAD_SIZE, HEAD_SIZE), HEAD_SIZE)
        k_cols = pl.ds(pl.multiple_of(hd + g * HEAD_SIZE, HEAD_SIZE), HEAD_SIZE)
        v_cols = pl.ds(pl.multiple_of(hd + (kv_heads + g) * HEAD_SIZE, HEAD_SIZE), HEAD_SIZE)
        q = gathered[full + (q_cols,)].reshape(rows, HEAD_SIZE).astype(F32)
        k = gathered[full + (k_cols,)].reshape(rows, HEAD_SIZE).astype(F32)
        v = gathered[full + (v_cols,)].reshape(rows, HEAD_SIZE).astype(F32)
        own = jnp.sum(q * k, axis=1, keepdims=True) * scale
        lse = jnp.where(hit, my_lse[h : h + 1, :], LOW)
        top = jnp.maximum(jnp.max(lse, axis=1, keepdims=True), own)
        share = jnp.exp(lse - top)
        fresh = jnp.exp(own - top)
        inverse = 1.0 / (jnp.sum(share, axis=1, keepdims=True) + fresh)
        mixed_in = jnp.dot(
            (share * inverse)[:, :pos].astype(BF16),
            my_table[:, h * HEAD_SIZE : (h + 1) * HEAD_SIZE],
            preferred_element_type=F32,
        )
        heads.append((mixed_in + v * (fresh * inverse)).astype(BF16))
    attention = jnp.concatenate(heads, axis=1) if per_dev > 1 else heads[0]

    loads[4].wait()

    def project(j, carry):
        cols = pl.ds(pl.multiple_of(j * tile, tile), tile)
        product = jnp.dot(attention, proj_v[:, cols], preferred_element_type=F32)
        part[full + (cols,)] = product.astype(BF16).reshape(2, chips, row_dev, tile)
        return carry

    cuts = [(slice(None), pl.ds(c0, w)) for c0, w in halves(model, LANES)]
    half_tiles = model // tile // 2

    def project_half(i):
        lax.fori_loop(i * half_tiles, (i + 1) * half_tiles, project, 0)

    scatter_sum(2, [(part, part_sib, part_ring, cuts)], project_half)

    loads[3].wait()
    mixed = (hidden_v[...].astype(F32) + part[0, 0].astype(F32)).astype(BF16).astype(F32)
    scale_row = lax.rsqrt(jnp.mean(mixed * mixed, axis=1, keepdims=True) + 1e-06)
    normed_all[0, 0] = (mixed * scale_row * gain_ref[...].astype(F32).reshape(1, model)).astype(BF16)
    gather(3, normed_all, cuts)

    all_gates = gathered[full + (pl.ds(hd + 2 * kv_width, LANES),)].reshape(rows, LANES).astype(F32)
    gate_lane = lax.rem(lax.broadcasted_iota(jnp.int32, (rows, LANES), 1), LANES // 2)
    gate = jnp.sum(jnp.where(gate_lane == me, all_gates, 0.0), axis=1, keepdims=True)
    loads[5].wait()
    loads[6].wait()
    ff_tile = 256

    def hidden_units(j, carry):
        cols = pl.ds(pl.multiple_of(j * ff_tile, ff_tile), ff_tile)
        tokens = normed_all[...].reshape(rows, model)
        gate_proj = jnp.dot(tokens, wg_v[:, cols], preferred_element_type=F32)
        up_proj = jnp.dot(tokens, wu_v[:, cols], preferred_element_type=F32)
        act_v[:, cols] = (jax.nn.silu(gate_proj) * up_proj).astype(BF16)
        return carry

    lax.fori_loop(0, ff // ff_tile, hidden_units, 0)
    loads[7].wait()

    def down(j, carry):
        cols = pl.ds(pl.multiple_of(j * tile, tile), tile)
        product = jnp.dot(act_v[...], wd_v[:, cols], preferred_element_type=F32)
        part[full + (cols,)] = (
            (product * gate).astype(BF16).reshape(2, chips, row_dev, tile)
        )
        return carry

    def down_half(i):
        lax.fori_loop(i * half_tiles, (i + 1) * half_tiles, down, 0)

    scatter_sum(4, [(part, part_sib, part_ring, cuts)], down_half)
    out_ref[...] = (mixed + part[0, 0].astype(F32)).astype(BF16)


def on_device(
    snake,
    hidden_in,
    queries,
    fresh_key_value,
    segment_key_cache,
    segment_value_cache,
    segment_owner_row,
    segment_length,
    expert_ids,
    gate_score,
    out_proj,
    norm_gain,
    w_gate,
    w_up,
    w_down,
):
    n = lax.axis_size("dev")
    chips = n // 2
    row_dev, model = hidden_in.shape
    segs, slots, kv_width = segment_key_cache.shape
    kv_heads = kv_width // HEAD_SIZE
    ff = w_gate.shape[2]
    per_dev = HQ // n
    rows = n * row_dev
    pos = rows + n
    pos_lanes = -(-pos // LANES) * LANES
    dims = (n, snake, row_dev, model, ff, segs, slots, kv_heads, per_dev, pos, pos_lanes)
    own_cols = per_dev * HEAD_SIZE
    hd = queries.shape[1]
    vmem = pl.BlockSpec(memory_space=pltpu.VMEM)
    hbm = pl.BlockSpec(memory_space=pl.ANY)
    return pl.pallas_call(
        functools.partial(layer_kernel, dims),
        out_shape=jax.ShapeDtypeStruct((row_dev, model), BF16),
        in_specs=[hbm, hbm, vmem, hbm, hbm] + [vmem] * 4 + [hbm, vmem, hbm, hbm, hbm],
        out_specs=vmem,
        scratch_shapes=[
            pltpu.VMEM(segment_key_cache.shape, BF16),
            pltpu.VMEM(segment_value_cache.shape, BF16),
            pltpu.VMEM(out_proj.shape, BF16),
            pltpu.VMEM(w_gate.shape[1:], BF16),
            pltpu.VMEM(w_up.shape[1:], BF16),
            pltpu.VMEM(w_down.shape[1:], BF16),
            pltpu.VMEM((row_dev, model), BF16),
            pltpu.SemaphoreType.DMA((8,)),
            pltpu.VMEM((2, chips, row_dev, hd + 2 * kv_width + LANES), BF16),
            pltpu.VMEM((segs, hd), BF16),
            pltpu.VMEM((segs, hd), F32),
            pltpu.VMEM((2, chips, pos, own_cols), BF16),
            pltpu.VMEM((chips, pos, own_cols), BF16),
            pltpu.VMEM((2, chips // 2 + 1, pos, own_cols), BF16),
            pltpu.VMEM((2, chips, 8, pos_lanes), F32),
            pltpu.VMEM((chips, 8, pos_lanes), F32),
            pltpu.VMEM((2, chips // 2 + 1, 8, pos_lanes), F32),
            pltpu.VMEM((2, chips, row_dev, model), BF16),
            pltpu.VMEM((chips, row_dev, model), BF16),
            pltpu.VMEM((2, chips // 2 + 1, row_dev, model), BF16),
            pltpu.VMEM((2, chips, row_dev, model), BF16),
            pltpu.VMEM((rows, ff), BF16),
            pltpu.SemaphoreType.DMA((5, 4, 4 + chips)),
            pltpu.SemaphoreType.DMA((5, 4, 4 + chips)),
        ],
        compiler_params=pltpu.CompilerParams(
            collective_id=0, has_side_effects=True, vmem_limit_bytes=60 * 2**20
        ),
        name="decode_layer",
    )(
        hidden_in,
        queries,
        fresh_key_value,
        segment_key_cache,
        segment_value_cache,
        segment_owner_row.reshape(1, segs),
        segment_length.reshape(1, segs),
        expert_ids.T,
        gate_score.T,
        out_proj,
        norm_gain,
        w_gate,
        w_up,
        w_down,
    )


def snake_ring(mesh):
    places = [getattr(d, "coords", None) for d in mesh.devices.reshape(-1, mesh.shape["dev"])[0]]
    if any(p is None for p in places):
        return False
    places = [tuple(p) for p in places[::2]]
    return len(places) > 2 and len({p[1] for p in places}) == 2 and len({p[2] for p in places}) > 1


def solution(mesh):
    placed = (
        P(("groups", "dev"), None),
        P(("groups", "dev"), None),
        P(("groups", "dev"), None, None),
        P(("groups", "dev"), None, None),
        P(("groups", "dev"), None, None),
        P(("groups", "dev")),
        P(("groups", "dev")),
        P(("groups", "dev"), None),
        P(("groups", "dev"), None),
        P("dev", None),
        P(),
        P("dev", None, None),
        P("dev", None, None),
        P("dev", None, None),
    )
    return jax.shard_map(
        functools.partial(on_device, snake_ring(mesh)),
        mesh=mesh,
        in_specs=placed,
        out_specs=P(("groups", "dev"), None),
        check_vma=False,
    )
```
